512 devices in a mesh: pipe: 4 (over z_lo), node: 8 (over z_hi, core), local: 16 (over x, y).
Axes of the slice: x: 4, y: 4, z: 16 (z_hi: 4, z_lo: 4; z = z_hi * 4 + z_lo), core: 2. Of those that a mesh axis runs over, the one named last changes fastest.
Arguments:
- next_grad: bfloat16 [4, 1024, 7168], P('pipe', ('node', 'local')), may hold values from -6 to 6
- routes: int32 [4, 1024, 4], P('pipe', ('node', 'local')), may hold values from 0 to 7, all different within a row; in each aligned block of 8 rows (0 to 7, 8 to 15, ..., all dimensions but the last counted through in order) at most 5 rows name the same one
- probs: bfloat16 [4, 1024, 4], P('pipe', ('node', 'local')), may hold values from 0.099609375 to 1
- down_weight: bfloat16 [4, 8, 2048, 7168], P('pipe', 'node', 'local'), may hold values from -0.0625 to 0.0625
- gate_pre: bfloat16 [4, 8, 640, 2048], P('pipe', 'node', None, 'local'), may hold values from -6 to 6
- up_pre: bfloat16 [4, 8, 640, 2048], P('pipe', 'node', None, 'local'), may hold values from -6 to 6
Outputs:
- gate_grad: bfloat16 [4, 8, 640, 2048], P('pipe', 'node', None, 'local')
- up_grad: bfloat16 [4, 8, 640, 2048], P('pipe', 'node', None, 'local')
- down_grad: bfloat16 [4, 8, 2048, 7168], P('pipe', 'node', 'local')
- prob_grad: float32 [4, 1024, 4], P('pipe', ('node', 'local'))
The draws below stay inside these ranges and needn't reach their ends.
Inputs may be any that keep to these rules, and one draw needn't show every extreme that they name: `routes`: each row names 4 different nodes; the tokens of one device name one node 5 times at most.
All inputs are finite; a program needn't handle non-finite values.
Results may differ from the reference program's by a relative error of at most 0.0049.
Values may be sent and summed in bfloat16 or wider, within the bound.
A program may use at most 128 MiB of HBM per device.

```python
import math
import jax
import jax.numpy as jnp
import numpy as np
from jax import lax

D = 7168
HE = 2048
TOK = 8
PICKS = 4
CAP = 5
EXPERTS = 8
TOKENS = 1024
SLOTS = 640
N_PIPE = 4
N_NODE = 8
N_LOCAL = 16


def block_levels(rng, shape, shards, smallest, top_value):
    gain, own = 1.0, jax.random.fold_in(rng, 6)
    for dim, parts in shards:
        steps = jnp.exp(jax.random.uniform(jax.random.fold_in(own, dim), (parts,), jnp.float32, smallest / len(shards), top_value / len(shards)))
        gain = gain * jnp.repeat(steps, shape[dim] // parts).reshape([-1 if axis == dim else 1 for axis in range(len(shape))])
    return gain


def routed_block(own_key, own, number, rows, amount, top, most, lean):
    ranking = jax.random.permutation(own_key, amount)
    heavy_load, ordinary = portions_of(amount, rows * top, most, lean, True), portions_of(amount, rows * top, most, lean, False)
    places = jnp.arange(amount)

    def named(tallies, turn):
        used = int((tallies > 0).sum())
        fixed = max(1, used // 4)
        shifted = fixed + (places - fixed + turn * (used - fixed)) % max(1, amount - fixed)
        return jnp.zeros((amount,), jnp.int32).at[ranking[jnp.where(places < fixed, places, shifted)]].set(jnp.asarray(tallies, jnp.int32))

    tallies = jnp.where(number % 4 == 0, named(heavy_load, number // 4), named(ordinary, number - number // 4 - 1))
    mixed = jax.random.permutation(jax.random.fold_in(own, 3), amount)
    giver, receiver = mixed[0:amount // 2 * 2:2], mixed[1:amount // 2 * 2:2]
    slack = jnp.minimum(tallies[giver] - 1, most - tallies[receiver]) // 2
    slack = jnp.where((giver == ranking[0]) | (receiver == ranking[0]) | (tallies[receiver] == 0), 0, jnp.maximum(slack, 0))
    shifted = jax.random.randint(jax.random.fold_in(own, 4), (amount // 2,), 0, 1 << 20) % (slack + 1)
    tallies = tallies.at[giver].add(-shifted).at[receiver].add(shifted)
    items = jnp.searchsorted(jnp.cumsum(tallies), jnp.arange(rows * top), side="right").astype(jnp.int32)
    table = items.reshape(top, rows).T
    table = table[jax.random.permutation(jax.random.fold_in(own, 1), rows)]
    turn = jax.random.randint(jax.random.fold_in(own, 2), (rows, 1), 0, top)
    return jnp.take_along_axis(table, (jnp.arange(top)[None, :] + turn) % top, axis=1)


def portions_of(number_of, total, limit, lean, full):
    weights = [(1 << 20) // math.isqrt(rank ** lean) + 1 for rank in range(1, number_of + 1)]
    largest = limit if full else min(limit, max(-(-total // number_of), total * weights[0] // sum(weights)))
    least = 1 if total - largest >= number_of - 1 else 0
    counts, rest = [largest] + [least] * (number_of - 1), total - largest - least * (number_of - 1)
    while rest > 0:
        movable = [i for i in range(1, number_of) if counts[i] < largest] or [i for i in range(1, number_of) if counts[i] < limit]
        pool, budget = sum([weights[i] for i in movable]), rest
        for i in movable:
            more = min(limit - counts[i], max(1, budget * weights[i] // pool), rest)
            counts[i] = counts[i] + more
            rest = rest - more
    return np.array(counts)


def normal_values(key, extent, deviation, bound, shards=(), held_as=jnp.bfloat16):
    loudness = block_levels(key, extent, shards, -0.22, 0.18) if shards else 1.0
    values = jax.random.normal(key, extent, jnp.float32) * deviation * loudness
    return jnp.minimum(jnp.maximum(values, -bound), bound).astype(held_as)


def setup_inputs(seed: int = 0) -> dict:
    key_list = jax.random.split(jax.random.key(seed), 7)
    next_grad = normal_values(key_list[0], (N_PIPE, TOKENS, D), 1.0, 6.0, ((0, 4), (1, 128)))
    routes_keys = jax.random.split(jax.random.fold_in(key_list[1], 1), N_PIPE * TOKENS // TOK)
    routes_turns = jax.random.permutation(jax.random.fold_in(key_list[1], 3), N_PIPE * TOKENS // TOK)
    routes = jax.vmap(lambda own, number: routed_block(jax.random.fold_in(key_list[1], 2), own, number, TOK, N_NODE, PICKS, CAP, 2))(routes_keys, routes_turns).reshape((N_PIPE, TOKENS, PICKS))
    probs = jnp.clip(jnp.exp(math.log(1.0) - 2.306499 * jax.random.uniform(key_list[2], (N_PIPE, TOKENS, PICKS), jnp.float32) ** block_levels(key_list[2], (N_PIPE, TOKENS, PICKS), ((0, 4), (1, 128)), -0.2, 0.2)), 0.099609375, 1.0).astype(jnp.bfloat16)
    down_weight = normal_values(key_list[3], (N_PIPE, EXPERTS, HE, D), D ** -0.5, 0.0625, ((0, 4), (1, 8), (2, 16)))
    gate_pre = normal_values(key_list[4], (N_PIPE, EXPERTS, SLOTS, HE), 1.5, 6.0, ((0, 4), (1, 8), (3, 16)))
    up_pre = normal_values(key_list[5], (N_PIPE, EXPERTS, SLOTS, HE), 1.0, 6.0, ((0, 4), (1, 8), (3, 16)))
    return dict(next_grad=next_grad, routes=routes, probs=probs, down_weight=down_weight, gate_pre=gate_pre, up_pre=up_pre)


def tables(route_rows, node_count, capacity):
    nodes = jnp.arange(node_count, dtype=jnp.int32)
    node_hits = (route_rows[:, :, None] == nodes[None, None, :]).astype(jnp.int32)
    picked = jnp.sum(node_hits, axis=1)
    earlier = jnp.cumsum(picked, axis=0) - picked
    places = jnp.arange(capacity, dtype=jnp.int32)
    select = (picked.T[:, None, :] == 1) & (earlier.T[:, None, :] == places[None, :, None])
    return node_hits, select


def expert_backward(slot_rows, slot_probs, gate_rows, up_rows, weight):
    scores = jnp.dot(slot_rows, weight.T, preferred_element_type=jnp.float32)
    gate_value = gate_rows.astype(jnp.float32)
    up_value = up_rows.astype(jnp.float32)
    gate_sig = jax.nn.sigmoid(gate_value)
    activated = gate_value * gate_sig
    hidden = activated * up_value
    partial_value = jnp.sum(hidden * scores, axis=1)
    weights = slot_probs.astype(jnp.float32)[:, None]
    hidden_grad = weights * scores
    d_gate = (hidden_grad * up_value * gate_sig * (1.0 + gate_value * (1.0 - gate_sig))).astype(jnp.bfloat16)
    d_up = (hidden_grad * activated).astype(jnp.bfloat16)
    scaled_hidden = (weights * hidden).astype(jnp.bfloat16)
    grad_w = jnp.dot(scaled_hidden.T, slot_rows, preferred_element_type=jnp.float32).astype(jnp.bfloat16)
    return partial_value, d_gate, d_up, grad_w


def reference(next_grad, routes, probs, down_weight, gate_pre, up_pre):
    groups = N_NODE * N_LOCAL
    high = lax.Precision.HIGHEST
    gate_all, up_all, down_all, prob_all = [], [], [], []
    for section in range(N_PIPE):
        incoming = next_grad[(section + 1) % N_PIPE].reshape(groups, TOK, D).astype(jnp.float32)
        route_rows = routes[section].reshape(groups, TOK, PICKS)
        prob_rows = probs[section].reshape(groups, TOK, PICKS).astype(jnp.float32)
        node_hits, select = jax.vmap(lambda r: tables(r, N_NODE, CAP))(route_rows)
        select_f = select.astype(jnp.float32)
        send_rows = jnp.einsum('jmct,jtd->jmcd', select_f, incoming, precision=high).astype(jnp.bfloat16)
        prob_at = jnp.sum(node_hits.astype(jnp.float32) * prob_rows[:, :, :, None], axis=2)
        send_probs = jnp.einsum('jmct,jtm->jmc', select_f, prob_at, precision=high).astype(jnp.bfloat16)
        routed = send_rows.reshape(N_NODE, N_LOCAL, N_NODE, CAP, D).transpose(2, 1, 0, 3, 4).reshape(N_NODE, SLOTS, D)
        slot_prob = send_probs.reshape(N_NODE, N_LOCAL, N_NODE, CAP).transpose(2, 1, 0, 3).reshape(N_NODE, SLOTS)
        partials, gates, ups, downs = [], [], [], []
        for expert in range(N_NODE):
            partial_value, d_gate, d_up, grad_w = expert_backward(routed[expert], slot_prob[expert], gate_pre[section, expert], up_pre[section, expert], down_weight[section, expert])
            partials.append(partial_value)
            gates.append(d_gate)
            ups.append(d_up)
            downs.append(grad_w)
        partial_all = jnp.stack(partials).reshape(N_NODE, N_LOCAL, N_NODE, CAP)
        returned = partial_all.transpose(2, 1, 0, 3).reshape(groups, N_NODE, CAP)
        value_at = jnp.einsum('jmct,jmc->jtm', select_f, returned, precision=high)
        grads = jnp.einsum('jtkm,jtm->jtk', node_hits.astype(jnp.float32), value_at, precision=high)
        prob_all.append(grads.reshape(TOKENS, PICKS))
        gate_all.append(jnp.stack(gates))
        up_all.append(jnp.stack(ups))
        down_all.append(jnp.stack(downs))
    return jnp.stack(gate_all), jnp.stack(up_all), jnp.stack(down_all), jnp.stack(prob_all)
```

```python
import functools

import jax
import jax.numpy as jnp
from jax import lax
from jax.experimental import pallas as pl
from jax.experimental.pallas import tpu as pltpu
from jax.sharding import PartitionSpec as P

MESH = pl.DeviceIdType.MESH
F32 = jnp.float32
BF16 = jnp.bfloat16
SIDE = 4
CAP = 5
TOK = 8
ROWS = 16
NT = (((1,), (1,)), ((), ()))


def kernel(
    sections,
    grad_ref,
    routes_ref,
    probs_ref,
    weight_hbm,
    gate_hbm,
    up_hbm,
    gate_out,
    up_out,
    down_out,
    prob_out,
    rows_buf,
    own_buf,
    weight_buf,
    pre_buf,
    pre_t,
    meta1,
    meta2,
    select,
    hid,
    gate_f,
    up_f,
    scaled,
    total,
    slot_total,
    slot_out,
    down_buf,
    part_send,
    part_recv,
    part2,
    z_recv,
    s1_recv,
    s2_recv,
    s3_recv,
    s4_recv,
    sib_recv,
    z_send,
    s1_send,
    s2_send,
    s3_send,
    s4_send,
    sib_send,
    meta_send,
    meta_recv,
    part_ssem,
    part_rsem,
    load_sem,
    store_sem,
):
    half = rows_buf.shape[-1]
    mid = half // 2
    quarter = mid // 2
    s = lax.axis_index("pipe")
    node = lax.axis_index("node")
    local = lax.axis_index("local")
    h, k = node // 2, lax.rem(node, 2)
    x, y = local // SIDE, lax.rem(local, SIDE)

    def ring(value):
        return lax.rem(value + 2 * SIDE, SIDE)

    def at(section, plane, core, px, py):
        return {"pipe": section, "node": plane * 2 + core, "local": px * SIDE + py}

    def remote(src, dst, ssem, rsem, device):
        return pltpu.make_async_remote_copy(
            src_ref=src, dst_ref=dst, send_sem=ssem, recv_sem=rsem, device_id=device, device_id_type=MESH
        )

    def send(ref, ssem, rsem, device):
        remote(ref, ref, ssem, rsem, device).start()

    def drain(ref, sem):
        pltpu.make_async_copy(ref, ref, sem).wait()

    s_up = lax.rem(s + 1, sections)
    s_down = lax.rem(s + sections - 1, sections)
    h_first = ring(h + jnp.where(s == sections - 1, 1, 0))
    h_back = ring(h - jnp.where(s == 0, 1, 0))

    line = y * 2 + k
    grid = h * SIDE + x

    def line_peer(j):
        other = lax.rem(line + j, 2 * SIDE)
        return at(s, h, lax.rem(other, 2), x, other // 2)

    def grid_peer(j):
        other = lax.rem(grid + j, SIDE * SIDE)
        return at(s, other // SIDE, k, lax.rem(other, SIDE), y)

    loads = [
        pltpu.make_async_copy(gate_hbm, pre_buf.at[0], load_sem.at[0]),
        pltpu.make_async_copy(up_hbm, pre_buf.at[1], load_sem.at[1]),
        pltpu.make_async_copy(weight_hbm.at[:, 0:half], weight_buf.at[0:128], load_sem.at[2]),
        pltpu.make_async_copy(weight_hbm.at[:, half : 2 * half], weight_buf.at[128:256], load_sem.at[3]),
    ]
    for load in loads:
        load.start()

    barrier = pltpu.get_barrier_semaphore()

    def greet(device):
        pl.semaphore_signal(barrier, inc=1, device_id=device, device_id_type=MESH)

    greet(at(s_up, h_first, k, x, y))
    greet(at(s_up, ring(h_first - 1), k, x, y))

    @pl.loop(1, 2 * SIDE)
    def _(j):
        greet(line_peer(j))

    @pl.loop(1, SIDE * SIDE)
    def _(j):
        greet(grid_peer(j))

    own_buf[0:TOK, :] = grad_ref[:, 0:half]
    own_buf[TOK:ROWS, :] = grad_ref[:, half : 2 * half]

    route_rows = routes_ref[...]
    prob_rows = probs_ref[...].astype(F32)
    lane = lax.broadcasted_iota(jnp.int32, (TOK, 128), 1)
    token = lax.broadcasted_iota(jnp.int32, (TOK, 128), 0)
    mine = lane - (y * 32 + k * ROWS) == token
    row16 = lax.broadcasted_iota(jnp.int32, (ROWS, 128), 0)
    tile = jnp.zeros((ROWS, 128), F32)
    for m in range(2 * SIDE):
        column = jnp.sum(jnp.where(route_rows == m, prob_rows, 0.0), axis=1, keepdims=True)
        row = jnp.sum(jnp.where(mine, column, 0.0), axis=0, keepdims=True)
        tile = tile + jnp.where(row16 == m, row, 0.0)
    meta1[line] = tile.astype(BF16)

    pl.semaphore_wait(barrier, 2 + (2 * SIDE - 1) + (SIDE * SIDE - 1))

    def z_copy(src, wave, hsrc, section, plane):
        return remote(
            src, rows_buf.at[hsrc, x, y, k], z_send.at[wave], z_recv.at[wave], at(section, plane, k, x, y)
        )

    z_copy(own_buf, 0, h, s_down, h_back).start()
    z_copy(own_buf, 1, h, s_down, ring(h_back + 1)).start()

    @pl.loop(1, 2 * SIDE)
    def _(j):
        send(meta1.at[line], meta_send.at[0], meta_recv.at[0], line_peer(j))

    def source(wave):
        return lax.rem(h_first + SIDE - wave, SIDE)

    def z_wait(wave):
        hw = source(wave)
        drain(rows_buf.at[hw, x, y, k], z_recv.at[wave])

    left, right = (0, mid), (mid, mid)

    def part(cols, piece):
        return pl.ds(cols[0] + piece * quarter, quarter)

    def row_blk(hw, px, cols):
        return rows_buf.at[hw, px, y, k, :, cols]

    def col_blk(hw, py, cols):
        return rows_buf.at[hw, x, py, k, :, cols]

    def row_set(hw, py, core, cols):
        return rows_buf.at[hw, :, py, core, :, cols]

    def col_set(hw, px, core, cols):
        return rows_buf.at[hw, px, :, core, :, cols]

    lcols, rcols = pl.ds(*left), pl.ds(*right)
    x_up, x_down, x_far = ring(x + 1), ring(x - 1), ring(x + 2)
    y_up, y_down, y_far = ring(y + 1), ring(y - 1), ring(y + 2)
    dev_x = (at(s, h, k, x_up, y), at(s, h, k, x_down, y))
    dev_y = (at(s, h, k, x, y_up), at(s, h, k, x, y_down))
    sibling = at(s, h, 1 - k, x, y)
    from_x, from_y = (x_down, x_up), (y_down, y_up)

    def step1(w):
        hw = source(w)
        for d in range(2):
            send(row_blk(hw, x, lcols), s1_send.at[w], s1_recv.at[w, d], dev_x[d])
            send(col_blk(hw, y, rcols), s1_send.at[w], s1_recv.at[w, 2 + d], dev_y[d])

    def step2(w):
        hw = source(w)
        for d in range(2):
            drain(row_blk(hw, from_x[d], lcols), s1_recv.at[w, d])
            send(row_blk(hw, from_x[d], part(left, d)), s2_send.at[w], s2_recv.at[w, 0], dev_x[d])
            drain(col_blk(hw, from_y[d], rcols), s1_recv.at[w, 2 + d])
            send(col_blk(hw, from_y[d], part(right, d)), s2_send.at[w], s2_recv.at[w, 1], dev_y[d])

    def step3(w):
        hw = source(w)
        drain(row_blk(hw, x_far, lcols), s2_recv.at[w, 0])
        for d in range(2):
            send(row_set(hw, y, k, lcols), s3_send.at[w], s3_recv.at[w, d], dev_y[d])
        drain(col_blk(hw, y_far, rcols), s2_recv.at[w, 1])
        for d in range(2):
            send(col_set(hw, x, k, rcols), s3_send.at[w], s3_recv.at[w, 2 + d], dev_x[d])
        hand(row_set(hw, y, k, lcols), w)
        hand(col_set(hw, x, k, rcols), w)

    def hand(ref, w):
        send(ref, sib_send.at[w], sib_recv.at[w], sibling)

    def step4(w):
        hw = source(w)
        for d in range(2):
            drain(row_set(hw, from_y[d], k, lcols), s3_recv.at[w, d])
            send(row_set(hw, from_y[d], k, part(left, d)), s4_send.at[w], s4_recv.at[w, 0], dev_y[d])
            drain(col_set(hw, from_x[d], k, rcols), s3_recv.at[w, 2 + d])
            send(col_set(hw, from_x[d], k, part(right, d)), s4_send.at[w], s4_recv.at[w, 1], dev_x[d])
        for d in range(2):
            hand(row_set(hw, from_y[d], k, lcols), w)
            hand(col_set(hw, from_x[d], k, rcols), w)

    def step5(w):
        hw = source(w)
        drain(row_set(hw, y_far, k, lcols), s4_recv.at[w, 0])
        hand(row_set(hw, y_far, k, lcols), w)
        drain(col_set(hw, x_far, k, rcols), s4_recv.at[w, 1])
        hand(col_set(hw, x_far, k, rcols), w)

    def arrived(w):
        drain(rows_buf.at[source(w), :, :, 1 - k], sib_recv.at[w])

    def sent(w):
        drain(rows_buf.at[0, 0, 0:2, 0], s1_send.at[w])
        drain(rows_buf.at[0, 0, 0, 0], s2_send.at[w])
        drain(rows_buf.at[0, 0:2, :, 0], s3_send.at[w])
        drain(rows_buf.at[0, 0, :, 0], s4_send.at[w])
        drain(rows_buf.at[0, :, :, 0], sib_send.at[w])

    z_wait(0)
    z_copy(rows_buf.at[h_first, x, y, k], 3, h_first, s, ring(h - 1)).start()
    step1(0)

    drain(meta1.at[0 : 2 * SIDE - 1], meta_recv.at[0])
    meta2[grid] = jnp.sum(meta1[...].astype(F32), axis=0).astype(BF16)

    @pl.loop(1, SIDE * SIDE)
    def _(j):
        send(meta2.at[grid], meta_send.at[1], meta_recv.at[1], grid_peer(j))

    step2(0)
    z_wait(1)
    z_copy(rows_buf.at[source(1), x, y, k], 2, source(1), s, ring(h + 1)).start()
    step3(0)
    step1(1)

    drain(meta2.at[0 : SIDE * SIDE - 1], meta_recv.at[1])
    for load in loads:
        load.wait()
    pre_t[...] = jnp.concatenate([pre_buf[0], pre_buf[1]], axis=1).astype(F32).T.astype(BF16)
    tokens = SIDE * 128
    slots = slot_total.shape[0]

    @pl.loop(0, SIDE)
    def _(hw):
        tiles = jnp.concatenate([meta2[hw * SIDE + j] for j in range(SIDE)], axis=1).astype(F32)
        rows = lax.broadcasted_iota(jnp.int32, (ROWS, tokens), 0)
        prob = jnp.sum(jnp.where(rows == node, tiles, 0.0), axis=0, keepdims=True)
        prob8 = jnp.broadcast_to(prob, (8, tokens))
        hit = jnp.where(prob8 > 0.0, 1.0, 0.0)
        at_lane = lax.broadcasted_iota(jnp.int32, (8, tokens), 1)
        place = lax.rem(at_lane, ROWS)
        rank = jnp.zeros((8, tokens), F32)
        for back in range(1, TOK):
            rank = rank + jnp.where(place >= back, pltpu.roll(hit, back, axis=1), 0.0)
        group = (at_lane // 32) * (2 * SIDE) + 2 * hw + lax.rem(at_lane // ROWS, 2)
        slot = jnp.where(prob8 > 0.0, group * CAP + rank.astype(jnp.int32), -1)[0:1]
        slot_row = lax.broadcasted_iota(jnp.int32, (slots, tokens), 0)
        select[hw] = jnp.where(slot_row == slot, 1.0, 0.0).astype(BF16)
        moved = jnp.dot(pre_t[...], select[hw], preferred_element_type=F32)
        gate, up = moved[0:128], moved[128:256]
        sig = 1.0 / (1.0 + jnp.exp(-gate))
        act = gate * sig
        hidden = act * up
        hid[hw] = hidden
        gate_f[hw] = prob * (up * sig * (1.0 + gate * (1.0 - sig)))
        up_f[hw] = prob * act
        scaled_hidden = prob * hidden
        scaled[hw, 0:128] = scaled_hidden.astype(BF16)
        scaled[hw, 128:256] = pltpu.roll(scaled_hidden, TOK, axis=1).astype(BF16)

    def compute(w):
        hw = source(w)

        @pl.loop(0, 2)
        def _(j):
            block = rows_buf[hw, pl.ds(2 * j, 2)].reshape(256, half)
            both = lax.dot_general(weight_buf[...], block, NT, preferred_element_type=F32)
            scores = both[0:128] + pltpu.roll(both[128:256], 256 - TOK, axis=1)
            cols = pl.ds(pl.multiple_of(j * 256, 256), 256)
            shares = jnp.sum((hid[hw, :, cols] * scores).reshape(ROWS, 8, 256), axis=0)
            part_send[hw, 2 * j] = shares[:, 0:128]
            part_send[hw, 2 * j + 1] = shares[:, 128:256]
            d_gate = (gate_f[hw, :, cols] * scores).astype(BF16)
            d_up = (up_f[hw, :, cols] * scores).astype(BF16)
            moved = lax.dot_general(
                select[hw, :, cols], jnp.concatenate([d_gate, d_up], axis=0), NT, preferred_element_type=F32
            )
            first = (w == 0) & (j == 0)

            @pl.when(first)
            def _():
                slot_total[...] = moved

            @pl.when(jnp.logical_not(first))
            def _():
                slot_total[...] += moved

        @pl.loop(0, SIDE)
        def _(px):
            own = (hw == h) & (px == x)

            @pl.when(own)
            def _():
                part_recv[grid] = part_send[hw, px]

            @pl.when(jnp.logical_not(own))
            def _():
                remote(
                    part_send.at[hw, px], part_recv.at[grid], part_ssem.at[0], part_rsem.at[0], at(s, hw, k, px, y)
                ).start()

        @pl.loop(0, half // 512)
        def _(c):
            cols = pl.ds(pl.multiple_of(c * 512, 512), 512)
            block = rows_buf[hw, :, :, :, :, cols].reshape(tokens, 512)
            more = jnp.dot(scaled[hw], block, preferred_element_type=F32)

            @pl.when(w == 0)
            def _():
                total[:, cols] = more

            @pl.when((w > 0) & (w < SIDE - 1))
            def _():
                total[:, cols] += more

            @pl.when(w == SIDE - 1)
            def _():
                down_buf[:, cols] = (total[:, cols] + more).astype(BF16)

    @pl.loop(0, SIDE + 1)
    def _(w):
        @pl.when(w > 0)
        def _():
            compute(w - 1)

        @pl.when(w < SIDE)
        def _():
            step4(w)

            @pl.when(w < SIDE - 1)
            def _():
                step2(w + 1)
                step3(w + 1)

            @pl.when(w < SIDE - 2)
            def _():
                z_wait(w + 2)
                step1(w + 2)

            step5(w)
            arrived(w)

    stores = [
        pltpu.make_async_copy(down_buf.at[0:128], down_out.at[:, 0:half], store_sem.at[0]),
        pltpu.make_async_copy(down_buf.at[128:256], down_out.at[:, half : 2 * half], store_sem.at[1]),
        pltpu.make_async_copy(slot_out.at[0], gate_out, store_sem.at[2]),
        pltpu.make_async_copy(slot_out.at[1], up_out, store_sem.at[3]),
    ]
    stores[0].start()
    stores[1].start()
    slot_out[0] = slot_total[:, 0:128].astype(BF16)
    slot_out[1] = slot_total[:, 128:256].astype(BF16)
    stores[2].start()
    stores[3].start()

    drain(part_recv.at[0 : SIDE * SIDE - 1], part_rsem.at[0])
    row8 = lax.broadcasted_iota(jnp.int32, (8, 128), 0)
    tile = jnp.zeros((8, 128), F32)
    for plane in range(SIDE):
        over_x = part_recv[plane * SIDE]
        for px in range(1, SIDE):
            over_x = over_x + part_recv[plane * SIDE + px]
        tile = tile + jnp.where(row8 == plane, jnp.sum(over_x, axis=0, keepdims=True), 0.0)
    part2[line] = tile

    @pl.loop(1, 2 * SIDE)
    def _(j):
        send(part2.at[line], part_ssem.at[1], part_rsem.at[1], line_peer(j))

    @pl.loop(0, SIDE)
    def _(w):
        sent(w)
        drain(rows_buf.at[0, 0, 0, 0], z_send.at[w])

    drain(meta1.at[0 : 2 * SIDE - 1], meta_send.at[0])
    drain(meta2.at[0 : SIDE * SIDE - 1], meta_send.at[1])
    drain(part_recv.at[0 : SIDE * SIDE - 1], part_ssem.at[0])

    drain(part2.at[0 : 2 * SIDE - 1], part_rsem.at[1])
    result = jnp.zeros((TOK, routes_ref.shape[1]), F32)
    for core in range(2):
        over_y = part2[core]
        for py in range(1, SIDE):
            over_y = over_y + part2[py * 2 + core]
        for plane in range(SIDE):
            column = jnp.sum(jnp.where(mine, over_y[plane : plane + 1], 0.0), axis=1, keepdims=True)
            result = result + jnp.where(route_rows == plane * 2 + core, column, 0.0)
    prob_out[...] = result
    drain(part2.at[0 : 2 * SIDE - 1], part_ssem.at[1])
    for store in stores:
        store.wait()


def shards(next_grad, routes, probs, down_weight, gate_pre, up_pre):
    sections = lax.axis_size("pipe")
    grad = next_grad[0]
    weight = down_weight[0, 0]
    gate_rows = gate_pre[0, 0]
    slots, hidden = gate_rows.shape
    width = grad.shape[1]
    half = width // 2
    tokens = SIDE * 128
    vmem = pl.BlockSpec(memory_space=pltpu.VMEM)
    hbm = pl.BlockSpec(memory_space=pl.ANY)
    dma = pltpu.SemaphoreType.DMA
    gate_grad, up_grad, down_grad, prob_grad = pl.pallas_call(
        functools.partial(kernel, sections),
        out_shape=(
            jax.ShapeDtypeStruct((slots, hidden), BF16),
            jax.ShapeDtypeStruct((slots, hidden), BF16),
            jax.ShapeDtypeStruct((hidden, width), BF16),
            jax.ShapeDtypeStruct(routes.shape[1:], F32),
        ),
        in_specs=[vmem, vmem, vmem, hbm, hbm, hbm],
        out_specs=(hbm, hbm, hbm, vmem),
        scratch_shapes=[
            pltpu.VMEM((SIDE, SIDE, SIDE, 2, ROWS, half), BF16),
            pltpu.VMEM((ROWS, half), BF16),
            pltpu.VMEM((2 * hidden, half), BF16),
            pltpu.VMEM((2, slots, hidden), BF16),
            pltpu.VMEM((2 * hidden, slots), BF16),
            pltpu.VMEM((2 * SIDE, ROWS, 128), BF16),
            pltpu.VMEM((SIDE * SIDE, ROWS, 128), BF16),
            pltpu.VMEM((SIDE, slots, tokens), BF16),
            pltpu.VMEM((SIDE, hidden, tokens), F32),
            pltpu.VMEM((SIDE, hidden, tokens), F32),
            pltpu.VMEM((SIDE, hidden, tokens), F32),
            pltpu.VMEM((SIDE, 2 * hidden, tokens), BF16),
            pltpu.VMEM((2 * hidden, half), F32),
            pltpu.VMEM((slots, 2 * hidden), F32),
            pltpu.VMEM((2, slots, hidden), BF16),
            pltpu.VMEM((2 * hidden, half), BF16),
            pltpu.VMEM((SIDE, SIDE, 8, 128), F32),
            pltpu.VMEM((SIDE * SIDE, 8, 128), F32),
            pltpu.VMEM((2 * SIDE, 8, 128), F32),
            dma((SIDE,)),
            dma((SIDE, 4)),
            dma((SIDE, 2)),
            dma((SIDE, 4)),
            dma((SIDE, 2)),
            dma((SIDE,)),
            dma((SIDE,)),
            dma((SIDE,)),
            dma((SIDE,)),
            dma((SIDE,)),
            dma((SIDE,)),
            dma((SIDE,)),
            dma((2,)),
            dma((2,)),
            dma((2,)),
            dma((2,)),
            dma((4,)),
            dma((4,)),
        ],
        compiler_params=pltpu.CompilerParams(
            collective_id=0, has_side_effects=True, vmem_limit_bytes=56 * 1024 * 1024
        ),
        cost_estimate=pl.CostEstimate(
            flops=4 * slots * hidden * width, bytes_accessed=4 * hidden * width, transcendentals=slots * hidden
        ),
    )(grad, routes[0], probs[0], weight, gate_rows, up_pre[0, 0])
    return (gate_grad[None, None], up_grad[None, None], down_grad[None, None], prob_grad[None])


def solution(mesh):
    return jax.shard_map(
        shards,
        mesh=mesh,
        in_specs=(
            P("pipe", ("node", "local"), None),
            P("pipe", ("node", "local"), None),
            P("pipe", ("node", "local"), None),
            P("pipe", "node", "local", None),
            P("pipe", "node", None, "local"),
            P("pipe", "node", None, "local"),
        ),
        out_specs=(
            P("pipe", "node", None, "local"),
            P("pipe", "node", None, "local"),
            P("pipe", "node", "local", None),
            P("pipe", ("node", "local"), None),
        ),
        check_vma=False,
    )
```

```python
import functools

import jax
import jax.numpy as jnp
from jax import lax
from jax.experimental import pallas as pl
from jax.experimental.pallas import tpu as pltpu
from jax.sharding import PartitionSpec as P

MESH = pl.DeviceIdType.MESH
F32 = jnp.float32
BF16 = jnp.bfloat16
SIDE = 4
CAP = 5
TOK = 8
ROWS = 16
NT = (((1,), (1,)), ((), ()))


def kernel(
    sections,
    grad_ref,
    routes_ref,
    probs_ref,
    weight_hbm,
    gate_hbm,
    up_hbm,
    slot_out,
    down_buf,
    prob_out,
    rows_buf,
    own_buf,
    weight_buf,
    pre_buf,
    pre_t,
    meta1,
    meta2,
    select,
    hid,
    gate_f,
    up_f,
    scaled,
    total,
    slot_total,
    part_send,
    part_recv,
    part2,
    z_recv,
    s1_recv,
    s2_recv,
    s3_recv,
    s4_recv,
    sib_recv,
    z_send,
    s1_send,
    s2_send,
    s3_send,
    s4_send,
    sib_send,
    meta_send,
    meta_recv,
    part_ssem,
    part_rsem,
    load_sem,
):
    half = rows_buf.shape[-1]
    mid = half // 2
    quarter = mid // 2
    s = lax.axis_index("pipe")
    node = lax.axis_index("node")
    local = lax.axis_index("local")
    h, k = node // 2, lax.rem(node, 2)
    x, y = local // SIDE, lax.rem(local, SIDE)

    def ring(value):
        return lax.rem(value + 2 * SIDE, SIDE)

    def at(section, plane, core, px, py):
        return {"pipe": section, "node": plane * 2 + core, "local": px * SIDE + py}

    def remote(src, dst, ssem, rsem, device):
        return pltpu.make_async_remote_copy(
            src_ref=src, dst_ref=dst, send_sem=ssem, recv_sem=rsem, device_id=device, device_id_type=MESH
        )

    def send(ref, ssem, rsem, device):
        remote(ref, ref, ssem, rsem, device).start()

    def drain(ref, sem):
        pltpu.make_async_copy(ref, ref, sem).wait()

    s_up = lax.rem(s + 1, sections)
    s_down = lax.rem(s + sections - 1, sections)
    h_first = ring(h + jnp.where(s == sections - 1, 1, 0))
    h_back = ring(h - jnp.where(s == 0, 1, 0))

    line = y * 2 + k
    grid = h * SIDE + x

    def line_peer(j):
        other = lax.rem(line + j, 2 * SIDE)
        return at(s, h, lax.rem(other, 2), x, other // 2)

    def grid_peer(j):
        other = lax.rem(grid + j, SIDE * SIDE)
        return at(s, other // SIDE, k, lax.rem(other, SIDE), y)

    loads = [
        pltpu.make_async_copy(gate_hbm, pre_buf.at[0], load_sem.at[0]),
        pltpu.make_async_copy(up_hbm, pre_buf.at[1], load_sem.at[1]),
        pltpu.make_async_copy(weight_hbm.at[:, 0:half], weight_buf.at[0:128], load_sem.at[2]),
        pltpu.make_async_copy(weight_hbm.at[:, half : 2 * half], weight_buf.at[128:256], load_sem.at[3]),
    ]
    for load in loads:
        load.start()

    barrier = pltpu.get_barrier_semaphore()

    def greet(device):
        pl.semaphore_signal(barrier, inc=1, device_id=device, device_id_type=MESH)

    greet(at(s_up, h_first, k, x, y))
    greet(at(s_up, ring(h_first - 1), k, x, y))

    @pl.loop(1, 2 * SIDE)
    def _(j):
        greet(line_peer(j))

    @pl.loop(1, SIDE * SIDE)
    def _(j):
        greet(grid_peer(j))

    own_buf[0:TOK, :] = grad_ref[:, 0:half]
    own_buf[TOK:ROWS, :] = grad_ref[:, half : 2 * half]

    base = y * 32 + k * ROWS
    lane = lax.broadcasted_iota(jnp.int32, (TOK, 128), 1)
    token = lax.broadcasted_iota(jnp.int32, (TOK, 128), 0)
    place_own = jnp.where(lane - base == token, 1.0, 0.0).astype(BF16)
    own_routes = jnp.dot(routes_ref[...].astype(F32).astype(BF16), place_own, preferred_element_type=F32)
    own_probs = jnp.dot(probs_ref[...], place_own, preferred_element_type=F32)
    picks = own_routes.shape[0]
    row16 = lax.broadcasted_iota(jnp.int32, (ROWS, 128), 0).astype(F32)
    tile = jnp.zeros((ROWS, 128), F32)
    for pick in range(picks):
        tile = tile + jnp.where(own_routes[pick : pick + 1] == row16, own_probs[pick : pick + 1], 0.0)
    meta1[line] = tile.astype(BF16)

    pl.semaphore_wait(barrier, 2 + (2 * SIDE - 1) + (SIDE * SIDE - 1))

    def z_copy(src, wave, hsrc, section, plane):
        return remote(
            src, rows_buf.at[hsrc, x, y, k], z_send.at[wave], z_recv.at[wave], at(section, plane, k, x, y)
        )

    z_copy(own_buf, 0, h, s_down, h_back).start()
    z_copy(own_buf, 1, h, s_down, ring(h_back + 1)).start()

    @pl.loop(1, 2 * SIDE)
    def _(j):
        send(meta1.at[line], meta_send.at[0], meta_recv.at[0], line_peer(j))

    swap = jnp.where(s == sections - 1, 1, 0)

    def offset(wave):
        return jnp.where(wave == 2, 2 + swap, jnp.where(wave == 3, 3 - swap, wave))

    def source(wave):
        return lax.rem(h_first + SIDE - offset(wave), SIDE)

    def z_wait(wave):
        hw = source(wave)
        drain(rows_buf.at[hw, x, y, k], z_recv.at[offset(wave)])

    left, right = (0, mid), (mid, mid)

    def part(cols, piece):
        return pl.ds(cols[0] + piece * quarter, quarter)

    def blk(hw, px, py, cols):
        return rows_buf.at[hw, px, py, k, :, cols]

    halves = (pl.ds(*left), pl.ds(*right))
    lcols, rcols = halves
    full = pl.ds(0, half)
    x_up, x_down, x_far = ring(x + 1), ring(x - 1), ring(x + 2)
    y_up, y_down, y_far = ring(y + 1), ring(y - 1), ring(y + 2)
    dev_x = (at(s, h, k, x_up, y), at(s, h, k, x_down, y))
    dev_y = (at(s, h, k, x, y_up), at(s, h, k, x, y_down))
    sibling = at(s, h, 1 - k, x, y)
    from_x, from_y = (x_down, x_up, x_far), (y_down, y_up, y_far)

    def hand(ref, w):
        send(ref, sib_send.at[w], sib_recv.at[w], sibling)

    def step1(w):
        mine = blk(source(w), x, y, full)
        for d in range(2):
            send(mine, s1_send.at[w], s1_recv.at[w, d], dev_x[d])
            send(mine, s1_send.at[w], s1_recv.at[w, 2 + d], dev_y[d])
        hand(mine, w)

    def step2(w):
        hw = source(w)
        for d in range(2):
            drain(blk(hw, from_x[d], y, full), s1_recv.at[w, d])
            send(blk(hw, from_x[d], y, halves[d]), s2_send.at[w], s2_recv.at[w, 0], dev_x[d])
            for e in range(2):
                send(blk(hw, from_x[d], y, lcols), s3_send.at[w], s3_recv.at[w, e, d], dev_y[e])
            drain(blk(hw, x, from_y[d], full), s1_recv.at[w, 2 + d])
            send(blk(hw, x, from_y[d], halves[d]), s2_send.at[w], s2_recv.at[w, 1], dev_y[d])
            for e in range(2):
                send(blk(hw, x, from_y[d], rcols), s3_send.at[w], s3_recv.at[w, 2 + e, d], dev_x[e])
        for d in range(2):
            hand(blk(hw, from_x[d], y, full), w)
            hand(blk(hw, x, from_y[d], full), w)

    def step3(w):
        hw = source(w)
        drain(blk(hw, x_far, y, full), s2_recv.at[w, 0])
        for e in range(2):
            send(blk(hw, x_far, y, lcols), s3_send.at[w], s3_recv.at[w, e, 2], dev_y[e])
        drain(blk(hw, x, y_far, full), s2_recv.at[w, 1])
        for e in range(2):
            send(blk(hw, x, y_far, rcols), s3_send.at[w], s3_recv.at[w, 2 + e, 2], dev_x[e])
        hand(blk(hw, x_far, y, full), w)
        hand(blk(hw, x, y_far, full), w)

    def step4(w):
        hw = source(w)
        for j in range(3):
            for e in range(2):
                drain(blk(hw, from_x[j], from_y[e], lcols), s3_recv.at[w, e, j])
                send(blk(hw, from_x[j], from_y[e], part(left, e)), s4_send.at[w], s4_recv.at[w, 0], dev_y[e])
                drain(blk(hw, from_x[e], from_y[j], rcols), s3_recv.at[w, 2 + e, j])
                send(blk(hw, from_x[e], from_y[j], part(right, e)), s4_send.at[w], s4_recv.at[w, 1], dev_x[e])
        for j in range(3):
            for e in range(2):
                hand(blk(hw, from_x[j], from_y[e], lcols), w)
                hand(blk(hw, from_x[e], from_y[j], rcols), w)

    def step5(w):
        hw = source(w)
        drain(rows_buf.at[hw, 0:3, y_far, k, :, lcols], s4_recv.at[w, 0])
        for j in range(3):
            hand(blk(hw, from_x[j], y_far, lcols), w)
        drain(rows_buf.at[hw, x_far, 0:3, k, :, rcols], s4_recv.at[w, 1])
        for j in range(3):
            hand(blk(hw, x_far, from_y[j], rcols), w)

    def arrived(w):
        drain(rows_buf.at[source(w), :, :, 1 - k], sib_recv.at[w])

    def sent(w):
        drain(rows_buf.at[0, 0, :, 0], s1_send.at[w])
        drain(rows_buf.at[0, 0, 0:2, 0], s2_send.at[w])
        drain(rows_buf.at[0, 0:3, 0:2, 0], s3_send.at[w])
        drain(rows_buf.at[0, 0, 0:3, 0], s4_send.at[w])
        drain(rows_buf.at[0, :, :, 0], sib_send.at[w])

    z_wait(0)
    z_copy(rows_buf.at[h_first, x, y, k], 3, h_first, s, ring(h - 1)).start()
    step1(0)

    drain(meta1.at[0 : 2 * SIDE - 1], meta_recv.at[0])
    meta2[grid] = jnp.sum(meta1[...].astype(F32), axis=0).astype(BF16)

    @pl.loop(1, SIDE * SIDE)
    def _(j):
        send(meta2.at[grid], meta_send.at[1], meta_recv.at[1], grid_peer(j))

    step2(0)
    z_wait(1)
    z_copy(rows_buf.at[source(1), x, y, k], 2, source(1), s, ring(h + 1)).start()
    step1(1)

    step3(0)
    step2(1)
    drain(meta2.at[0 : SIDE * SIDE - 1], meta_recv.at[1])
    for load in loads:
        load.wait()
    pre_t[...] = jnp.concatenate([pre_buf[0], pre_buf[1]], axis=1).astype(F32).T.astype(BF16)
    tokens = SIDE * 128
    slots = slot_total.shape[0]

    def prepare(w):
        hw = source(w)
        tiles = jnp.concatenate([meta2[hw * SIDE + j] for j in range(SIDE)], axis=1).astype(F32)
        rows = lax.broadcasted_iota(jnp.int32, (ROWS, tokens), 0)
        prob = jnp.sum(jnp.where(rows == node, tiles, 0.0), axis=0, keepdims=True)
        prob8 = jnp.broadcast_to(prob, (8, tokens))
        hit = jnp.where(prob8 > 0.0, 1.0, 0.0)
        at_lane = lax.broadcasted_iota(jnp.int32, (8, tokens), 1)
        place = lax.rem(at_lane, ROWS)
        rank = jnp.zeros((8, tokens), F32)
        for back in range(1, TOK):
            rank = rank + jnp.where(place >= back, pltpu.roll(hit, back, axis=1), 0.0)
        group = (at_lane // 32) * (2 * SIDE) + 2 * hw + lax.rem(at_lane // ROWS, 2)
        slot = jnp.where(prob8 > 0.0, group * CAP + rank.astype(jnp.int32), -1)[0:1]
        slot_row = lax.broadcasted_iota(jnp.int32, (slots, tokens), 0)
        select[hw] = jnp.where(slot_row == slot, 1.0, 0.0).astype(BF16)
        moved = jnp.dot(pre_t[...], select[hw], preferred_element_type=F32)
        gate, up = moved[0:128], moved[128:256]
        sig = 1.0 / (1.0 + jnp.exp(-gate))
        act = gate * sig
        hidden = act * up
        hid[hw] = hidden
        gate_f[hw] = prob * (up * sig * (1.0 + gate * (1.0 - sig)))
        up_f[hw] = prob * act
        scaled_hidden = prob * hidden
        scaled[hw, 0:128] = scaled_hidden.astype(BF16)
        scaled[hw, 128:256] = pltpu.roll(scaled_hidden, TOK, axis=1).astype(BF16)

    def scores_of(w, j):
        hw = source(w)
        block = rows_buf[hw, pl.ds(2 * j, 2)].reshape(256, half)
        both = lax.dot_general(weight_buf[...], block, NT, preferred_element_type=F32)
        scores = both[0:128] + pltpu.roll(both[128:256], 256 - TOK, axis=1)
        cols = pl.ds(j * 256, 256)
        shares = jnp.sum((hid[hw, :, cols] * scores).reshape(ROWS, 8, 256), axis=0)
        part_send[hw, 2 * j] = shares[:, 0:128]
        part_send[hw, 2 * j + 1] = shares[:, 128:256]
        d_gate = (gate_f[hw, :, cols] * scores).astype(BF16)
        d_up = (up_f[hw, :, cols] * scores).astype(BF16)
        moved = lax.dot_general(
            select[hw, :, cols], jnp.concatenate([d_gate, d_up], axis=0), NT, preferred_element_type=F32
        )
        if j == 0:

            @pl.when(w == 0)
            def _():
                slot_total[...] = moved

            @pl.when(w > 0)
            def _():
                slot_total[...] += moved

        else:
            slot_total[...] += moved

    def share(w):
        hw = source(w)

        @pl.loop(0, SIDE)
        def _(px):
            own = (hw == h) & (px == x)

            @pl.when(own)
            def _():
                part_recv[grid] = part_send[hw, px]

            @pl.when(jnp.logical_not(own))
            def _():
                remote(
                    part_send.at[hw, px], part_recv.at[grid], part_ssem.at[0], part_rsem.at[0], at(s, hw, k, px, y)
                ).start()

    def down_of(w, low, high, last):
        hw = source(w)

        @pl.loop(low, high)
        def _(c):
            cols = pl.ds(pl.multiple_of(c * 512, 512), 512)
            block = rows_buf[hw, :, :, :, :, cols].reshape(tokens, 512)
            more = jnp.dot(scaled[hw], block, preferred_element_type=F32)
            if last:
                down_buf[:, cols] = (total[:, cols] + more).astype(BF16)
            else:

                @pl.when(w == 0)
                def _():
                    total[:, cols] = more

                @pl.when(w > 0)
                def _():
                    total[:, cols] += more

    tiles_of_down = half // 512
    prepare(0)
    step4(0)
    z_wait(2)
    step1(2)

    @pl.loop(1, SIDE)
    def _(w):
        step3(w)
        step5(w - 1)

        @pl.when(w < SIDE - 1)
        def _():
            step2(w + 1)

        prepare(w)
        arrived(w - 1)
        scores_of(w - 1, 0)
        step4(w)

        @pl.when(w < SIDE - 2)
        def _():
            z_wait(w + 2)
            step1(w + 2)

        scores_of(w - 1, 1)
        share(w - 1)
        down_of(w - 1, 0, tiles_of_down, False)

    step5(SIDE - 1)
    arrived(SIDE - 1)
    scores_of(SIDE - 1, 0)
    scores_of(SIDE - 1, 1)
    share(SIDE - 1)
    down_of(SIDE - 1, 0, tiles_of_down, True)
    slot_out[0] = slot_total[:, 0:128].astype(BF16)
    slot_out[1] = slot_total[:, 128:256].astype(BF16)

    drain(part_recv.at[0 : SIDE * SIDE - 1], part_rsem.at[0])
    row8 = lax.broadcasted_iota(jnp.int32, (8, 128), 0)
    tile = jnp.zeros((8, 128), F32)
    for plane in range(SIDE):
        over_x = part_recv[plane * SIDE]
        for px in range(1, SIDE):
            over_x = over_x + part_recv[plane * SIDE + px]
        tile = tile + jnp.where(row8 == plane, jnp.sum(over_x, axis=0, keepdims=True), 0.0)
    part2[line] = tile

    @pl.loop(1, 2 * SIDE)
    def _(j):
        send(part2.at[line], part_ssem.at[1], part_rsem.at[1], line_peer(j))

    @pl.loop(0, SIDE)
    def _(w):
        sent(w)
        drain(rows_buf.at[0, 0, 0, 0], z_send.at[w])

    drain(meta1.at[0 : 2 * SIDE - 1], meta_send.at[0])
    drain(meta2.at[0 : SIDE * SIDE - 1], meta_send.at[1])
    drain(part_recv.at[0 : SIDE * SIDE - 1], part_ssem.at[0])

    drain(part2.at[0 : 2 * SIDE - 1], part_rsem.at[1])
    result = jnp.zeros((8, 128), F32)
    row8f = row8.astype(F32)
    for pick in range(picks):
        for core in range(2):
            over_y = part2[core]
            for py in range(1, SIDE):
                over_y = over_y + part2[py * 2 + core]
            chosen = jnp.where(own_routes[pick : pick + 1] == row8f * 2.0 + core, over_y, 0.0)
            result = result + jnp.where(row8 == pick, jnp.sum(chosen, axis=0, keepdims=True), 0.0)
    prob_out[...] = pltpu.roll(result, lax.rem(128 - base, 128), axis=1)[0:picks, 0:TOK]
    drain(part2.at[0 : 2 * SIDE - 1], part_ssem.at[1])


def publish(slot_in, down_in, prob_in, gate_out, up_out, down_out, prob_out, sem):
    half = down_in.shape[1]
    hidden = down_in.shape[0] // 2
    moves = [
        pltpu.make_async_copy(down_in.at[0:hidden], down_out.at[:, 0:half], sem.at[0]),
        pltpu.make_async_copy(down_in.at[hidden : 2 * hidden], down_out.at[:, half : 2 * half], sem.at[1]),
        pltpu.make_async_copy(slot_in.at[0], gate_out, sem.at[2]),
        pltpu.make_async_copy(slot_in.at[1], up_out, sem.at[3]),
        pltpu.make_async_copy(prob_in, prob_out, sem.at[4]),
    ]
    for move in moves:
        move.start()
    for move in moves:
        move.wait()


def shards(next_grad, routes, probs, down_weight, gate_pre, up_pre):
    sections = lax.axis_size("pipe")
    grad = next_grad[0]
    weight = down_weight[0, 0]
    gate_rows = gate_pre[0, 0]
    slots, hidden = gate_rows.shape
    width = grad.shape[1]
    picks = routes.shape[2]
    half = width // 2
    tokens = SIDE * 128
    vmem = pl.BlockSpec(memory_space=pltpu.VMEM)
    hbm = pl.BlockSpec(memory_space=pl.ANY)
    dma = pltpu.SemaphoreType.DMA
    slot_grads, down_halves, prob_t = pl.pallas_call(
        functools.partial(kernel, sections),
        out_shape=(
            pltpu.VMEM((2, slots, hidden), BF16),
            pltpu.VMEM((2 * hidden, half), BF16),
            pltpu.VMEM((picks, TOK), F32),
        ),
        in_specs=[vmem, vmem, vmem, hbm, hbm, hbm],
        out_specs=(vmem, vmem, vmem),
        scratch_shapes=[
            pltpu.VMEM((SIDE, SIDE, SIDE, 2, ROWS, half), BF16),
            pltpu.VMEM((ROWS, half), BF16),
            pltpu.VMEM((2 * hidden, half), BF16),
            pltpu.VMEM((2, slots, hidden), BF16),
            pltpu.VMEM((2 * hidden, slots), BF16),
            pltpu.VMEM((2 * SIDE, ROWS, 128), BF16),
            pltpu.VMEM((SIDE * SIDE, ROWS, 128), BF16),
            pltpu.VMEM((SIDE, slots, tokens), BF16),
            pltpu.VMEM((SIDE, hidden, tokens), F32),
            pltpu.VMEM((SIDE, hidden, tokens), F32),
            pltpu.VMEM((SIDE, hidden, tokens), F32),
            pltpu.VMEM((SIDE, 2 * hidden, tokens), BF16),
            pltpu.VMEM((2 * hidden, half), F32),
            pltpu.VMEM((slots, 2 * hidden), F32),
            pltpu.VMEM((SIDE, SIDE, 8, 128), F32),
            pltpu.VMEM((SIDE * SIDE, 8, 128), F32),
            pltpu.VMEM((2 * SIDE, 8, 128), F32),
            dma((SIDE,)),
            dma((SIDE, 4)),
            dma((SIDE, 2)),
            dma((SIDE, 4, 3)),
            dma((SIDE, 2)),
            dma((SIDE,)),
            dma((SIDE,)),
            dma((SIDE,)),
            dma((SIDE,)),
            dma((SIDE,)),
            dma((SIDE,)),
            dma((SIDE,)),
            dma((2,)),
            dma((2,)),
            dma((2,)),
            dma((2,)),
            dma((4,)),
        ],
        compiler_params=pltpu.CompilerParams(
            collective_id=0, has_side_effects=True, vmem_limit_bytes=52 * 1024 * 1024
        ),
        cost_estimate=pl.CostEstimate(
            flops=4 * slots * hidden * width, bytes_accessed=4 * hidden * width, transcendentals=slots * hidden
        ),
    )(grad, routes[0].T, probs[0].T, weight, gate_rows, up_pre[0, 0])
    gate_grad, up_grad, down_grad, prob_grad = pl.pallas_call(
        publish,
        out_shape=(
            jax.ShapeDtypeStruct((slots, hidden), BF16),
            jax.ShapeDtypeStruct((slots, hidden), BF16),
            jax.ShapeDtypeStruct((hidden, width), BF16),
            jax.ShapeDtypeStruct((picks, TOK), F32),
        ),
        in_specs=[vmem, vmem, vmem],
        out_specs=(hbm, hbm, hbm, hbm),
        scratch_shapes=[dma((5,))],
    )(slot_grads, down_halves, prob_t)
    return (gate_grad[None, None], up_grad[None, None], down_grad[None, None], prob_grad.T[None])


def solution(mesh):
    return jax.shard_map(
        shards,
        mesh=mesh,
        in_specs=(
            P("pipe", ("node", "local"), None),
            P("pipe", ("node", "local"), None),
            P("pipe", ("node", "local"), None),
            P("pipe", "node", "local", None),
            P("pipe", "node", None, "local"),
            P("pipe", "node", None, "local"),
        ),
        out_specs=(
            P("pipe", "node", None, "local"),
            P("pipe", "node", None, "local"),
            P("pipe", "node", "local", None),
            P("pipe", ("node", "local"), None),
        ),
        check_vma=False,
    )
```

```python
import functools

import jax
import jax.numpy as jnp
from jax import lax
from jax.experimental import pallas as pl
from jax.experimental.pallas import tpu as pltpu
from jax.sharding import PartitionSpec as P

MESH = pl.DeviceIdType.MESH
F32 = jnp.float32
BF16 = jnp.bfloat16
SIDE = 4
CAP = 5
TOK = 8
ROWS = 16
NT = (((1,), (1,)), ((), ()))


def kernel(
    sections,
    grad_ref,
    routes_ref,
    probs_ref,
    weight_hbm,
    gate_hbm,
    up_hbm,
    slot_out,
    down_buf,
    prob_out,
    rows_buf,
    own_buf,
    weight_buf,
    pre_buf,
    pre_t,
    meta1,
    meta2,
    select,
    hid,
    gate_f,
    up_f,
    scaled,
    total,
    slot_total,
    part_send,
    part_recv,
    z_recv,
    s1_recv,
    s2_recv,
    s3_recv,
    s4_recv,
    sib_recv,
    z_send,
    s1_send,
    s2_send,
    s3_send,
    s4_send,
    sib_send,
    meta_send,
    meta_recv,
    part_ssem,
    part_rsem,
    load_sem,
):
    half = rows_buf.shape[-1]
    mid = half // 2
    quarter = mid // 2
    s = lax.axis_index("pipe")
    node = lax.axis_index("node")
    local = lax.axis_index("local")
    h, k = node // 2, lax.rem(node, 2)
    x, y = local // SIDE, lax.rem(local, SIDE)

    def ring(value):
        return lax.rem(value + 2 * SIDE, SIDE)

    def at(section, plane, core, px, py):
        return {"pipe": section, "node": plane * 2 + core, "local": px * SIDE + py}

    def remote(src, dst, ssem, rsem, device):
        return pltpu.make_async_remote_copy(
            src_ref=src, dst_ref=dst, send_sem=ssem, recv_sem=rsem, device_id=device, device_id_type=MESH
        )

    def send(ref, ssem, rsem, device):
        remote(ref, ref, ssem, rsem, device).start()

    def drain(ref, sem):
        pltpu.make_async_copy(ref, ref, sem).wait()

    s_up = lax.rem(s + 1, sections)
    s_down = lax.rem(s + sections - 1, sections)
    h_first = ring(h + jnp.where(s == sections - 1, 1, 0))
    h_back = ring(h - jnp.where(s == 0, 1, 0))

    line = y * 2 + k
    me = node * SIDE * SIDE + local
    grid = h * SIDE + x

    def line_peer(j):
        other = lax.rem(line + j, 2 * SIDE)
        return at(s, h, lax.rem(other, 2), x, other // 2)

    def grid_peer(j):
        other = lax.rem(grid + j, SIDE * SIDE)
        return at(s, other // SIDE, k, lax.rem(other, SIDE), y)

    loads = [
        pltpu.make_async_copy(gate_hbm, pre_buf.at[0], load_sem.at[0]),
        pltpu.make_async_copy(up_hbm, pre_buf.at[1], load_sem.at[1]),
        pltpu.make_async_copy(weight_hbm.at[:, 0:half], weight_buf.at[0:128], load_sem.at[2]),
        pltpu.make_async_copy(weight_hbm.at[:, half : 2 * half], weight_buf.at[128:256], load_sem.at[3]),
    ]
    for load in loads:
        load.start()

    barrier = pltpu.get_barrier_semaphore()

    def greet(device):
        pl.semaphore_signal(barrier, inc=1, device_id=device, device_id_type=MESH)

    greet(at(s_up, h_first, k, x, y))
    greet(at(s_up, ring(h_first - 1), k, x, y))

    @pl.loop(1, 2 * SIDE)
    def _(j):
        greet(line_peer(j))

    @pl.loop(1, SIDE * SIDE)
    def _(j):
        greet(grid_peer(j))

    own_buf[0:TOK, :] = grad_ref[:, 0:half]
    own_buf[TOK:ROWS, :] = grad_ref[:, half : 2 * half]

    base = y * 32 + k * ROWS
    lane = lax.broadcasted_iota(jnp.int32, (TOK, 128), 1)
    token = lax.broadcasted_iota(jnp.int32, (TOK, 128), 0)
    place_own = jnp.where(lane - base == token, 1.0, 0.0).astype(BF16)
    own_routes = jnp.dot(routes_ref[...].astype(F32).astype(BF16), place_own, preferred_element_type=F32)
    own_probs = jnp.dot(probs_ref[...], place_own, preferred_element_type=F32)
    picks = own_routes.shape[0]
    row16 = lax.broadcasted_iota(jnp.int32, (ROWS, 128), 0).astype(F32)
    tile = jnp.zeros((ROWS, 128), F32)
    for pick in range(picks):
        tile = tile + jnp.where(own_routes[pick : pick + 1] == row16, own_probs[pick : pick + 1], 0.0)
    meta1[line] = tile.astype(BF16)

    pl.semaphore_wait(barrier, 2 + (2 * SIDE - 1) + (SIDE * SIDE - 1))

    def z_copy(src, wave, hsrc, section, plane):
        return remote(
            src, rows_buf.at[hsrc, x, y, k], z_send.at[wave], z_recv.at[wave], at(section, plane, k, x, y)
        )

    z_copy(own_buf, 0, h, s_down, h_back).start()
    z_copy(own_buf, 1, h, s_down, ring(h_back + 1)).start()

    @pl.loop(1, 2 * SIDE)
    def _(j):
        send(meta1.at[line], meta_send.at[0], meta_recv.at[0], line_peer(j))

    swap = jnp.where(s == sections - 1, 1, 0)

    def offset(wave):
        return jnp.where(wave == 2, 2 + swap, jnp.where(wave == 3, 3 - swap, wave))

    def source(wave):
        return lax.rem(h_first + SIDE - offset(wave), SIDE)

    def z_wait(wave):
        hw = source(wave)
        drain(rows_buf.at[hw, x, y, k], z_recv.at[offset(wave)])

    left, right = (0, mid), (mid, mid)

    def part(cols, piece):
        return pl.ds(cols[0] + piece * quarter, quarter)

    def blk(hw, px, py, cols):
        return rows_buf.at[hw, px, py, k, :, cols]

    halves = (pl.ds(*left), pl.ds(*right))
    lcols, rcols = halves
    full = pl.ds(0, half)
    x_up, x_down, x_far = ring(x + 1), ring(x - 1), ring(x + 2)
    y_up, y_down, y_far = ring(y + 1), ring(y - 1), ring(y + 2)
    dev_x = (at(s, h, k, x_up, y), at(s, h, k, x_down, y))
    dev_y = (at(s, h, k, x, y_up), at(s, h, k, x, y_down))
    sibling = at(s, h, 1 - k, x, y)
    from_x, from_y = (x_down, x_up, x_far), (y_down, y_up, y_far)

    def hand(ref, w):
        send(ref, sib_send.at[w], sib_recv.at[w], sibling)

    def step1(w):
        mine = blk(source(w), x, y, full)
        for d in range(2):
            send(mine, s1_send.at[w], s1_recv.at[w, d], dev_x[d])
            send(mine, s1_send.at[w], s1_recv.at[w, 2 + d], dev_y[d])
        hand(mine, w)

    def step2(w):
        hw = source(w)
        for d in range(2):
            drain(blk(hw, from_x[d], y, full), s1_recv.at[w, d])
            send(blk(hw, from_x[d], y, halves[d]), s2_send.at[w], s2_recv.at[w, 0], dev_x[d])
            for e in range(2):
                send(blk(hw, from_x[d], y, lcols), s3_send.at[w], s3_recv.at[w, e, d], dev_y[e])
            drain(blk(hw, x, from_y[d], full), s1_recv.at[w, 2 + d])
            send(blk(hw, x, from_y[d], halves[d]), s2_send.at[w], s2_recv.at[w, 1], dev_y[d])
            for e in range(2):
                send(blk(hw, x, from_y[d], rcols), s3_send.at[w], s3_recv.at[w, 2 + e, d], dev_x[e])
        for d in range(2):
            hand(blk(hw, from_x[d], y, full), w)
            hand(blk(hw, x, from_y[d], full), w)

    def step3(w):
        hw = source(w)
        drain(blk(hw, x_far, y, full), s2_recv.at[w, 0])
        for e in range(2):
            send(blk(hw, x_far, y, lcols), s3_send.at[w], s3_recv.at[w, e, 2], dev_y[e])
        drain(blk(hw, x, y_far, full), s2_recv.at[w, 1])
        for e in range(2):
            send(blk(hw, x, y_far, rcols), s3_send.at[w], s3_recv.at[w, 2 + e, 2], dev_x[e])
        hand(blk(hw, x_far, y, full), w)
        hand(blk(hw, x, y_far, full), w)

    def step4(w):
        hw = source(w)
        for j in range(3):
            for e in range(2):
                drain(blk(hw, from_x[j], from_y[e], lcols), s3_recv.at[w, e, j])
                send(blk(hw, from_x[j], from_y[e], part(left, e)), s4_send.at[w], s4_recv.at[w, 0], dev_y[e])
                drain(blk(hw, from_x[e], from_y[j], rcols), s3_recv.at[w, 2 + e, j])
                send(blk(hw, from_x[e], from_y[j], part(right, e)), s4_send.at[w], s4_recv.at[w, 1], dev_x[e])
        for j in range(3):
            for e in range(2):
                hand(blk(hw, from_x[j], from_y[e], lcols), w)
                hand(blk(hw, from_x[e], from_y[j], rcols), w)

    def step5(w):
        hw = source(w)
        drain(rows_buf.at[hw, 0:3, y_far, k, :, lcols], s4_recv.at[w, 0])
        for j in range(3):
            hand(blk(hw, from_x[j], y_far, lcols), w)
        drain(rows_buf.at[hw, x_far, 0:3, k, :, rcols], s4_recv.at[w, 1])
        for j in range(3):
            hand(blk(hw, x_far, from_y[j], rcols), w)

    def arrived(w):
        drain(rows_buf.at[source(w), :, :, 1 - k], sib_recv.at[w])

    def sent(w):
        drain(rows_buf.at[0, 0, :, 0], s1_send.at[w])
        drain(rows_buf.at[0, 0, 0:2, 0], s2_send.at[w])
        drain(rows_buf.at[0, 0:3, 0:2, 0], s3_send.at[w])
        drain(rows_buf.at[0, 0, 0:3, 0], s4_send.at[w])
        drain(rows_buf.at[0, :, :, 0], sib_send.at[w])

    z_wait(0)
    z_copy(rows_buf.at[h_first, x, y, k], 3, h_first, s, ring(h - 1)).start()
    step1(0)

    drain(meta1.at[0 : 2 * SIDE - 1], meta_recv.at[0])
    meta2[grid] = jnp.sum(meta1[...].astype(F32), axis=0).astype(BF16)

    @pl.loop(1, SIDE * SIDE)
    def _(j):
        send(meta2.at[grid], meta_send.at[1], meta_recv.at[1], grid_peer(j))

    step2(0)
    z_wait(1)
    z_copy(rows_buf.at[source(1), x, y, k], 2, source(1), s, ring(h + 1)).start()
    step1(1)

    step3(0)
    step2(1)
    drain(meta2.at[0 : SIDE * SIDE - 1], meta_recv.at[1])
    for load in loads:
        load.wait()
    pre_t[...] = jnp.concatenate([pre_buf[0], pre_buf[1]], axis=1).astype(F32).T.astype(BF16)
    tokens = SIDE * 128
    slots = slot_total.shape[0]

    def prepare(w):
        hw = source(w)
        tiles = jnp.concatenate([meta2[hw * SIDE + j] for j in range(SIDE)], axis=1).astype(F32)
        rows = lax.broadcasted_iota(jnp.int32, (ROWS, tokens), 0)
        prob = jnp.sum(jnp.where(rows == node, tiles, 0.0), axis=0, keepdims=True)
        prob8 = jnp.broadcast_to(prob, (8, tokens))
        hit = jnp.where(prob8 > 0.0, 1.0, 0.0)
        at_lane = lax.broadcasted_iota(jnp.int32, (8, tokens), 1)
        place = lax.rem(at_lane, ROWS)
        rank = jnp.zeros((8, tokens), F32)
        for back in range(1, TOK):
            rank = rank + jnp.where(place >= back, pltpu.roll(hit, back, axis=1), 0.0)
        group = (at_lane // 32) * (2 * SIDE) + 2 * hw + lax.rem(at_lane // ROWS, 2)
        slot = jnp.where(prob8 > 0.0, group * CAP + rank.astype(jnp.int32), -1)[0:1]
        slot_row = lax.broadcasted_iota(jnp.int32, (slots, tokens), 0)
        select[hw] = jnp.where(slot_row == slot, 1.0, 0.0).astype(BF16)
        moved = jnp.dot(pre_t[...], select[hw], preferred_element_type=F32)
        gate, up = moved[0:128], moved[128:256]
        sig = 1.0 / (1.0 + jnp.exp(-gate))
        act = gate * sig
        hidden = act * up
        hid[hw] = hidden
        gate_f[hw] = prob * (up * sig * (1.0 + gate * (1.0 - sig)))
        up_f[hw] = prob * act
        scaled_hidden = prob * hidden
        scaled[hw, 0:128] = scaled_hidden.astype(BF16)
        scaled[hw, 128:256] = pltpu.roll(scaled_hidden, TOK, axis=1).astype(BF16)

    def scores_of(w, j):
        hw = source(w)
        block = rows_buf[hw, pl.ds(2 * j, 2)].reshape(256, half)
        both = lax.dot_general(weight_buf[...], block, NT, preferred_element_type=F32)
        scores = both[0:128] + pltpu.roll(both[128:256], 256 - TOK, axis=1)
        cols = pl.ds(j * 256, 256)
        shares = jnp.sum(hid[hw, :, cols] * scores, axis=0, keepdims=True)
        part_send[hw, 2 * j] = shares[:, 0:128]
        part_send[hw, 2 * j + 1] = shares[:, 128:256]
        d_gate = (gate_f[hw, :, cols] * scores).astype(BF16)
        d_up = (up_f[hw, :, cols] * scores).astype(BF16)
        moved = lax.dot_general(
            select[hw, :, cols], jnp.concatenate([d_gate, d_up], axis=0), NT, preferred_element_type=F32
        )
        if j == 0:

            @pl.when(w == 0)
            def _():
                slot_total[...] = moved

            @pl.when(w > 0)
            def _():
                slot_total[...] += moved

        else:
            slot_total[...] += moved

    def share(w):
        hw = source(w)

        @pl.loop(0, 8 * SIDE)
        def _(j):
            px, py, core = j // 8, lax.rem(j // 2, SIDE), lax.rem(j, 2)
            own = (hw == h) & (px == x) & (py == y) & (core == k)

            @pl.when(own)
            def _():
                part_recv[me] = part_send[hw, px]

            @pl.when(jnp.logical_not(own))
            def _():
                remote(
                    part_send.at[hw, px], part_recv.at[me], part_ssem.at[0], part_rsem.at[0], at(s, hw, core, px, py)
                ).start()

    def down_of(w, low, high, last):
        hw = source(w)

        @pl.loop(low, high)
        def _(c):
            cols = pl.ds(pl.multiple_of(c * 512, 512), 512)
            block = rows_buf[hw, :, :, :, :, cols].reshape(tokens, 512)
            more = jnp.dot(scaled[hw], block, preferred_element_type=F32)
            if last:
                down_buf[:, cols] = (total[:, cols] + more).astype(BF16)
            else:

                @pl.when(w == 0)
                def _():
                    total[:, cols] = more

                @pl.when(w > 0)
                def _():
                    total[:, cols] += more

    tiles_of_down = half // 512
    prepare(0)
    step4(0)
    z_wait(2)
    step1(2)

    @pl.loop(1, SIDE)
    def _(w):
        step3(w)
        step5(w - 1)

        @pl.when(w < SIDE - 1)
        def _():
            step2(w + 1)

        prepare(w)
        arrived(w - 1)
        scores_of(w - 1, 0)
        step4(w)

        @pl.when(w < SIDE - 2)
        def _():
            z_wait(w + 2)
            step1(w + 2)

        scores_of(w - 1, 1)
        share(w - 1)
        down_of(w - 1, 0, tiles_of_down, False)

    step5(SIDE - 1)
    arrived(SIDE - 1)
    scores_of(SIDE - 1, 0)
    scores_of(SIDE - 1, 1)
    share(SIDE - 1)
    down_of(SIDE - 1, 0, tiles_of_down, True)
    slot_out[0] = slot_total[:, 0:128].astype(BF16)
    slot_out[1] = slot_total[:, 128:256].astype(BF16)

    @pl.loop(0, SIDE)
    def _(w):
        sent(w)
        drain(rows_buf.at[0, 0, 0, 0], z_send.at[w])

    drain(meta1.at[0 : 2 * SIDE - 1], meta_send.at[0])
    drain(meta2.at[0 : SIDE * SIDE - 1], meta_send.at[1])

    others = part_recv.at[0 : part_recv.shape[0] - 1]
    drain(others, part_ssem.at[0])
    drain(others, part_rsem.at[0])
    row8 = lax.broadcasted_iota(jnp.int32, (8, 128), 0)
    result = jnp.zeros((8, 128), F32)
    for m in range(2 * SIDE):
        share_sum = part_recv[m * SIDE * SIDE]
        for j in range(1, SIDE * SIDE):
            share_sum = share_sum + part_recv[m * SIDE * SIDE + j]
        for pick in range(picks):
            chosen = jnp.where(own_routes[pick : pick + 1] == m, share_sum, 0.0)
            result = result + jnp.where(row8 == pick, chosen, 0.0)
    prob_out[...] = pltpu.roll(result, lax.rem(128 - base, 128), axis=1)[0:picks, 0:TOK]


def publish(slot_in, down_in, prob_in, gate_out, up_out, down_out, prob_out, sem):
    half = down_in.shape[1]
    hidden = down_in.shape[0] // 2
    moves = [
        pltpu.make_async_copy(down_in.at[0:hidden], down_out.at[:, 0:half], sem.at[0]),
        pltpu.make_async_copy(down_in.at[hidden : 2 * hidden], down_out.at[:, half : 2 * half], sem.at[1]),
        pltpu.make_async_copy(slot_in.at[0], gate_out, sem.at[2]),
        pltpu.make_async_copy(slot_in.at[1], up_out, sem.at[3]),
        pltpu.make_async_copy(prob_in, prob_out, sem.at[4]),
    ]
    for move in moves:
        move.start()
    for move in moves:
        move.wait()


def shards(next_grad, routes, probs, down_weight, gate_pre, up_pre):
    sections = lax.axis_size("pipe")
    grad = next_grad[0]
    weight = down_weight[0, 0]
    gate_rows = gate_pre[0, 0]
    slots, hidden = gate_rows.shape
    width = grad.shape[1]
    picks = routes.shape[2]
    half = width // 2
    tokens = SIDE * 128
    vmem = pl.BlockSpec(memory_space=pltpu.VMEM)
    hbm = pl.BlockSpec(memory_space=pl.ANY)
    dma = pltpu.SemaphoreType.DMA
    slot_grads, down_halves, prob_t = pl.pallas_call(
        functools.partial(kernel, sections),
        out_shape=(
            pltpu.VMEM((2, slots, hidden), BF16),
            pltpu.VMEM((2 * hidden, half), BF16),
            pltpu.VMEM((picks, TOK), F32),
        ),
        in_specs=[vmem, vmem, vmem, hbm, hbm, hbm],
        out_specs=(vmem, vmem, vmem),
        scratch_shapes=[
            pltpu.VMEM((SIDE, SIDE, SIDE, 2, ROWS, half), BF16),
            pltpu.VMEM((ROWS, half), BF16),
            pltpu.VMEM((2 * hidden, half), BF16),
            pltpu.VMEM((2, slots, hidden), BF16),
            pltpu.VMEM((2 * hidden, slots), BF16),
            pltpu.VMEM((2 * SIDE, ROWS, 128), BF16),
            pltpu.VMEM((SIDE * SIDE, ROWS, 128), BF16),
            pltpu.VMEM((SIDE, slots, tokens), BF16),
            pltpu.VMEM((SIDE, hidden, tokens), F32),
            pltpu.VMEM((SIDE, hidden, tokens), F32),
            pltpu.VMEM((SIDE, hidden, tokens), F32),
            pltpu.VMEM((SIDE, 2 * hidden, tokens), BF16),
            pltpu.VMEM((2 * hidden, half), F32),
            pltpu.VMEM((slots, 2 * hidden), F32),
            pltpu.VMEM((SIDE, SIDE, 1, 128), F32),
            pltpu.VMEM((2 * SIDE * SIDE * SIDE, 1, 128), F32),
            dma((SIDE,)),
            dma((SIDE, 4)),
            dma((SIDE, 2)),
            dma((SIDE, 4, 3)),
            dma((SIDE, 2)),
            dma((SIDE,)),
            dma((SIDE,)),
            dma((SIDE,)),
            dma((SIDE,)),
            dma((SIDE,)),
            dma((SIDE,)),
            dma((SIDE,)),
            dma((2,)),
            dma((2,)),
            dma((1,)),
            dma((1,)),
            dma((4,)),
        ],
        compiler_params=pltpu.CompilerParams(
            collective_id=0, has_side_effects=True, vmem_limit_bytes=52 * 1024 * 1024
        ),
        cost_estimate=pl.CostEstimate(
            flops=4 * slots * hidden * width, bytes_accessed=4 * hidden * width, transcendentals=slots * hidden
        ),
    )(grad, routes[0].T, probs[0].T, weight, gate_rows, up_pre[0, 0])
    gate_grad, up_grad, down_grad, prob_grad = pl.pallas_call(
        publish,
        out_shape=(
            jax.ShapeDtypeStruct((slots, hidden), BF16),
            jax.ShapeDtypeStruct((slots, hidden), BF16),
            jax.ShapeDtypeStruct((hidden, width), BF16),
            jax.ShapeDtypeStruct((picks, TOK), F32),
        ),
        in_specs=[vmem, vmem, vmem],
        out_specs=(hbm, hbm, hbm, hbm),
        scratch_shapes=[dma((5,))],
        compiler_params=pltpu.CompilerParams(vmem_limit_bytes=1024 * 1024),
    )(slot_grads, down_halves, prob_t)
    return (gate_grad[None, None], up_grad[None, None], down_grad[None, None], prob_grad.T[None])


def solution(mesh):
    return jax.shard_map(
        shards,
        mesh=mesh,
        in_specs=(
            P("pipe", ("node", "local"), None),
            P("pipe", ("node", "local"), None),
            P("pipe", ("node", "local"), None),
            P("pipe", "node", "local", None),
            P("pipe", "node", None, "local"),
            P("pipe", "node", None, "local"),
        ),
        out_specs=(
            P("pipe", "node", None, "local"),
            P("pipe", "node", None, "local"),
            P("pipe", "node", "local", None),
            P("pipe", ("node", "local"), None),
        ),
        check_vma=False,
    )
```

```python
import functools

import jax
import jax.numpy as jnp
from jax import lax
from jax.experimental import pallas as pl
from jax.experimental.pallas import tpu as pltpu
from jax.sharding import PartitionSpec as P

MESH = pl.DeviceIdType.MESH
F32 = jnp.float32
BF16 = jnp.bfloat16
SIDE = 4
CAP = 5
TOK = 8
ROWS = 16
NT = (((1,), (1,)), ((), ()))


def kernel(
    sections,
    grad_ref,
    routes_ref,
    probs_ref,
    weight_hbm,
    gate_hbm,
    up_hbm,
    slot_out,
    down_buf,
    prob_out,
    rows_buf,
    own_buf,
    far_buf,
    weight_buf,
    pre_buf,
    pre_t,
    meta1,
    meta2,
    select,
    hid,
    gate_f,
    up_f,
    scaled,
    total,
    slot_total,
    score_buf,
    part_send,
    part_recv,
    z_recv,
    s1_recv,
    s2_recv,
    s3_recv,
    s4_recv,
    sib_recv,
    z_send,
    s1_send,
    s2_send,
    s3_send,
    s4_send,
    sib_send,
    meta_send,
    meta_recv,
    part_ssem,
    part_rsem,
    load_sem,
    far_sem,
    far_send,
    far_recv,
):
    half = rows_buf.shape[-1]
    mid = half // 2
    quarter = mid // 2
    s = lax.axis_index("pipe")
    node = lax.axis_index("node")
    local = lax.axis_index("local")
    h, k = node // 2, lax.rem(node, 2)
    x, y = local // SIDE, lax.rem(local, SIDE)

    def ring(value):
        return lax.rem(value + 2 * SIDE, SIDE)

    def at(section, plane, core, px, py):
        return {"pipe": section, "node": plane * 2 + core, "local": px * SIDE + py}

    def remote(src, dst, ssem, rsem, device):
        return pltpu.make_async_remote_copy(
            src_ref=src, dst_ref=dst, send_sem=ssem, recv_sem=rsem, device_id=device, device_id_type=MESH
        )

    def send(ref, ssem, rsem, device):
        remote(ref, ref, ssem, rsem, device).start()

    def drain(ref, sem):
        pltpu.make_async_copy(ref, ref, sem).wait()

    s_up = lax.rem(s + 1, sections)
    s_down = lax.rem(s + sections - 1, sections)
    h_first = ring(h + jnp.where(s == sections - 1, 1, 0))
    h_back = ring(h - jnp.where(s == 0, 1, 0))

    line = y * 2 + k
    me = node * SIDE * SIDE + local
    grid = h * SIDE + x

    def line_peer(j):
        other = lax.rem(line + j, 2 * SIDE)
        return at(s, h, lax.rem(other, 2), x, other // 2)

    def plane_peer(j):
        return at(s, h, k, ring(x + j), y)

    planes = (at(s, ring(h + 1), k, x, y), at(s, ring(h - 1), k, x, y))

    barrier = pltpu.get_barrier_semaphore()

    def greet(device):
        pl.semaphore_signal(barrier, inc=1, device_id=device, device_id_type=MESH)

    greet(at(s_up, h_first, k, x, y))
    greet(at(s_up, ring(h_first - 1), k, x, y))

    @pl.loop(1, 2 * SIDE)
    def _(j):
        greet(line_peer(j))

    for j in range(1, SIDE):
        greet(plane_peer(j))
    for device in planes:
        greet(device)
    diagonal = at(s, h, k, ring(x + 2), ring(y + 2))
    greet(diagonal)

    own_buf[0:TOK, :] = grad_ref[:, 0:half]
    own_buf[TOK:ROWS, :] = grad_ref[:, half : 2 * half]

    pl.semaphore_wait(barrier, 2 + (2 * SIDE - 1) + (SIDE - 1) + 2 + 1)

    def z_copy(src, wave, hsrc, section, plane):
        return remote(
            src, rows_buf.at[hsrc, x, y, k], z_send.at[wave], z_recv.at[wave], at(section, plane, k, x, y)
        )

    halves = (pl.ds(0, mid), pl.ds(mid, mid))
    for i in range(2):
        remote(
            own_buf.at[:, halves[i]],
            rows_buf.at[h, x, y, k, :, halves[i]],
            z_send.at[0],
            z_recv.at[SIDE * i],
            at(s_down, h_back, k, x, y),
        ).start()
    z_copy(own_buf, 1, h, s_down, ring(h_back + 1)).start()
    remote(own_buf, far_buf, far_sem.at[0], far_sem.at[1], diagonal).start()

    loads = [
        pltpu.make_async_copy(gate_hbm, pre_buf.at[0], load_sem.at[0]),
        pltpu.make_async_copy(up_hbm, pre_buf.at[1], load_sem.at[1]),
        pltpu.make_async_copy(weight_hbm.at[:, 0:half], weight_buf.at[0:128], load_sem.at[2]),
        pltpu.make_async_copy(weight_hbm.at[:, half : 2 * half], weight_buf.at[128:256], load_sem.at[3]),
    ]
    for load in loads:
        load.start()

    base = y * 32 + k * ROWS
    lane = lax.broadcasted_iota(jnp.int32, (TOK, 128), 1)
    token = lax.broadcasted_iota(jnp.int32, (TOK, 128), 0)
    place_own = jnp.where(lane - base == token, 1.0, 0.0).astype(BF16)
    own_routes = jnp.dot(routes_ref[...].astype(F32).astype(BF16), place_own, preferred_element_type=F32)
    own_probs = jnp.dot(probs_ref[...], place_own, preferred_element_type=F32)
    picks = own_routes.shape[0]
    row16 = lax.broadcasted_iota(jnp.int32, (ROWS, 128), 0).astype(F32)
    tile = jnp.zeros((ROWS, 128), F32)
    for pick in range(picks):
        tile = tile + jnp.where(own_routes[pick : pick + 1] == row16, own_probs[pick : pick + 1], 0.0)
    meta1[line] = tile.astype(BF16)

    @pl.loop(1, 2 * SIDE)
    def _(j):
        send(meta1.at[line], meta_send.at[0], meta_recv.at[0], line_peer(j))

    swap = jnp.where(s == sections - 1, 1, 0)

    def offset(wave):
        return jnp.where(wave == 2, 2 + swap, jnp.where(wave == 3, 3 - swap, wave))

    def source(wave):
        return lax.rem(h_first + SIDE - offset(wave), SIDE)

    def z_wait(wave):
        hw = source(wave)
        drain(rows_buf.at[hw, x, y, k], z_recv.at[offset(wave)])

    left, right = (0, mid), (mid, mid)

    def part(cols, piece):
        return pl.ds(cols[0] + piece * quarter, quarter)

    def blk(hw, px, py, cols):
        return rows_buf.at[hw, px, py, k, :, cols]

    lcols, rcols = halves
    full = pl.ds(0, half)
    x_up, x_down, x_far = ring(x + 1), ring(x - 1), ring(x + 2)
    y_up, y_down, y_far = ring(y + 1), ring(y - 1), ring(y + 2)
    dev_x = (at(s, h, k, x_up, y), at(s, h, k, x_down, y))
    dev_y = (at(s, h, k, x, y_up), at(s, h, k, x, y_down))
    sibling = at(s, h, 1 - k, x, y)
    from_x, from_y = (x_down, x_up, x_far), (y_down, y_up, y_far)

    def hand(ref, w):
        send(ref, sib_send.at[w], sib_recv.at[w], sibling)

    def step1(w, cols):
        mine = blk(source(w), x, y, cols)
        for d in range(2):
            send(mine, s1_send.at[w], s1_recv.at[w, d], dev_x[d])
            send(mine, s1_send.at[w], s1_recv.at[w, 2 + d], dev_y[d])

    def step2(w):
        hw = source(w)
        for d in range(2):
            drain(blk(hw, from_x[d], y, full), s1_recv.at[w, d])
            send(blk(hw, from_x[d], y, halves[d]), s2_send.at[w], s2_recv.at[w, 0], dev_x[d])
            for e in range(2):
                send(blk(hw, from_x[d], y, lcols), s3_send.at[w], s3_recv.at[w, e, d], dev_y[e])
            drain(blk(hw, x, from_y[d], full), s1_recv.at[w, 2 + d])
            send(blk(hw, x, from_y[d], halves[d]), s2_send.at[w], s2_recv.at[w, 1], dev_y[d])
            for e in range(2):
                send(blk(hw, x, from_y[d], rcols), s3_send.at[w], s3_recv.at[w, 2 + e, d], dev_x[e])
        for d in range(2):
            hand(blk(hw, from_x[d], y, full), w)
            hand(blk(hw, x, from_y[d], full), w)

    def step3(w):
        hw = source(w)
        drain(blk(hw, x_far, y, full), s2_recv.at[w, 0])
        for e in range(2):
            send(blk(hw, x_far, y, lcols), s3_send.at[w], s3_recv.at[w, e, 2], dev_y[e])
        drain(blk(hw, x, y_far, full), s2_recv.at[w, 1])
        for e in range(2):
            send(blk(hw, x, y_far, rcols), s3_send.at[w], s3_recv.at[w, 2 + e, 2], dev_x[e])
        hand(blk(hw, x_far, y, full), w)
        hand(blk(hw, x, y_far, full), w)

    def step4(w):
        hw = source(w)
        for j in range(2):
            for e in range(2):
                drain(blk(hw, from_x[j], from_y[e], lcols), s3_recv.at[w, e, j])
                send(blk(hw, from_x[j], from_y[e], part(left, e)), s4_send.at[w], s4_recv.at[w, 0], dev_y[e])
                drain(blk(hw, from_x[e], from_y[j], rcols), s3_recv.at[w, 2 + e, j])
                send(blk(hw, from_x[e], from_y[j], part(right, e)), s4_send.at[w], s4_recv.at[w, 1], dev_x[e])
        hand(blk(hw, x, y, full), w)
        for j in range(2):
            for e in range(2):
                hand(blk(hw, from_x[j], from_y[e], lcols), w)
                hand(blk(hw, from_x[e], from_y[j], rcols), w)

    def step5(w):
        hw = source(w)
        for e in range(2):
            drain(blk(hw, x_far, from_y[e], lcols), s3_recv.at[w, e, 2])
            hand(blk(hw, x_far, from_y[e], lcols), w)
            drain(blk(hw, from_x[e], y_far, rcols), s3_recv.at[w, 2 + e, 2])
            hand(blk(hw, from_x[e], y_far, rcols), w)
        drain(rows_buf.at[hw, 0:2, y_far, k, :, lcols], s4_recv.at[w, 0])
        drain(rows_buf.at[hw, x_far, 0:2, k, :, rcols], s4_recv.at[w, 1])
        for j in range(2):
            hand(blk(hw, from_x[j], y_far, lcols), w)
            hand(blk(hw, x_far, from_y[j], rcols), w)

    def far_copy(src, index, hsrc, section, plane):
        return remote(
            src,
            rows_buf.at[hsrc, x_far, y_far, k],
            far_send.at[index],
            far_recv.at[index],
            at(section, plane, k, x, y),
        )

    def far_wait(w):
        hw = source(w)
        drain(rows_buf.at[hw, x_far, y_far, k], far_recv.at[offset(w)])
        hand(rows_buf.at[hw, x_far, y_far, k], w)

    def arrived(w):
        drain(rows_buf.at[source(w), :, :, 1 - k], sib_recv.at[w])

    def sent(w):
        drain(rows_buf.at[0, 0, :, 0], s1_send.at[w])
        drain(rows_buf.at[0, 0, 0:2, 0], s2_send.at[w])
        drain(rows_buf.at[0, 0:3, 0:2, 0], s3_send.at[w])
        drain(rows_buf.at[0, 0, 0:2, 0], s4_send.at[w])
        drain(rows_buf.at[0, :, :, 0], sib_send.at[w])

    for i in range(2):
        drain(rows_buf.at[h_first, x, y, k, :, halves[i]], z_recv.at[SIDE * i])
        step1(0, halves[i])
    z_copy(rows_buf.at[h_first, x, y, k], 3, h_first, s, ring(h - 1)).start()

    drain(meta1.at[0 : 2 * SIDE - 1], meta_recv.at[0])
    meta2[grid] = jnp.sum(meta1[...].astype(F32), axis=0).astype(BF16)

    def pass_on(tile, kind):
        for j in range(1, SIDE):
            send(meta2.at[tile], meta_send.at[1], meta_recv.at[kind], plane_peer(j))

    above, below, across = ring(h + 1) * SIDE + x, ring(h - 1) * SIDE + x, ring(h + 2) * SIDE + x
    for device in planes:
        send(meta2.at[grid], meta_send.at[1], meta_recv.at[1], device)
    pass_on(grid, 2)
    drain(far_buf, far_sem.at[1])
    far_copy(far_buf, 0, h, s_down, h_back).start()
    far_copy(far_buf, 1, h, s_down, ring(h_back + 1)).start()
    step2(0)
    drain(meta2.at[0:2], meta_recv.at[1])
    send(meta2.at[below], meta_send.at[1], meta_recv.at[3], planes[0])
    pass_on(above, 4)
    pass_on(below, 4)
    z_wait(1)
    z_copy(rows_buf.at[source(1), x, y, k], 2, source(1), s, ring(h + 1)).start()
    step1(1, full)

    step3(0)
    step2(1)
    drain(meta2.at[0], meta_recv.at[3])
    pass_on(across, 5)
    drain(meta2.at[0 : SIDE - 1], meta_recv.at[2])
    drain(meta2.at[0 : 2 * SIDE - 2], meta_recv.at[4])
    for load in loads:
        load.wait()
    pre_t[...] = jnp.concatenate([pre_buf[0], pre_buf[1]], axis=1).astype(F32).T.astype(BF16)
    tokens = SIDE * 128
    slots = slot_total.shape[0]

    def prepare(w):
        hw = source(w)
        tiles = jnp.concatenate([meta2[hw * SIDE + j] for j in range(SIDE)], axis=1).astype(F32)
        rows = lax.broadcasted_iota(jnp.int32, (ROWS, tokens), 0)
        prob = jnp.sum(jnp.where(rows == node, tiles, 0.0), axis=0, keepdims=True)
        prob8 = jnp.broadcast_to(prob, (8, tokens))
        hit = jnp.where(prob8 > 0.0, 1.0, 0.0)
        at_lane = lax.broadcasted_iota(jnp.int32, (8, tokens), 1)
        place = lax.rem(at_lane, ROWS)
        rank = jnp.zeros((8, tokens), F32)
        for back in range(1, TOK):
            rank = rank + jnp.where(place >= back, pltpu.roll(hit, back, axis=1), 0.0)
        group = (at_lane // 32) * (2 * SIDE) + 2 * hw + lax.rem(at_lane // ROWS, 2)
        slot = jnp.where(prob8 > 0.0, group * CAP + rank.astype(jnp.int32), -1)[0:1]
        slot_row = lax.broadcasted_iota(jnp.int32, (slots, tokens), 0)
        select[hw] = jnp.where(slot_row == slot, 1.0, 0.0).astype(BF16)
        moved = jnp.dot(pre_t[...], select[hw], preferred_element_type=F32)
        gate, up = moved[0:128], moved[128:256]
        sig = 1.0 / (1.0 + jnp.exp(-gate))
        act = gate * sig
        hidden = act * up
        hid[hw] = hidden
        gate_f[hw] = prob * (up * sig * (1.0 + gate * (1.0 - sig)))
        up_f[hw] = prob * act
        scaled_hidden = prob * hidden
        scaled[hw, 0:128] = scaled_hidden.astype(BF16)
        scaled[hw, 128:256] = pltpu.roll(scaled_hidden, TOK, axis=1).astype(BF16)

    def scores_of(w, j):
        hw = source(w)
        block = rows_buf[hw, pl.ds(2 * j, 2)].reshape(256, half)
        both = lax.dot_general(weight_buf[...], block, NT, preferred_element_type=F32)
        scores = both[0:128] + pltpu.roll(both[128:256], 256 - TOK, axis=1)
        cols = pl.ds(j * 256, 256)
        shares = jnp.sum(hid[hw, :, cols] * scores, axis=0, keepdims=True)
        part_send[hw, 2 * j] = shares[:, 0:128]
        part_send[hw, 2 * j + 1] = shares[:, 128:256]
        score_buf[hw, :, cols] = scores

    def share(w, j):
        hw = source(w)
        for px in (2 * j, 2 * j + 1):
            for py in range(SIDE):
                for core in range(2):
                    own = (hw == h) & (px == x) & (py == y) & (core == k)

                    @pl.when(own)
                    def _():
                        part_recv[me] = part_send[hw, px]

                    @pl.when(jnp.logical_not(own))
                    def _():
                        remote(
                            part_send.at[hw, px],
                            part_recv.at[me],
                            part_ssem.at[0],
                            part_rsem.at[0],
                            at(s, hw, core, px, py),
                        ).start()

    def grads_of(w):
        hw = source(w)
        d_gate = (gate_f[hw] * score_buf[hw]).astype(BF16)
        d_up = (up_f[hw] * score_buf[hw]).astype(BF16)
        moved = lax.dot_general(
            select[hw], jnp.concatenate([d_gate, d_up], axis=0), NT, preferred_element_type=F32
        )

        @pl.when(w == 0)
        def _():
            slot_total[...] = moved

        @pl.when(w > 0)
        def _():
            slot_total[...] += moved

    def down_of(w, last):
        hw, after = source(w), source(w + 1)
        step = mid

        @pl.loop(0, half // step)
        def _(c):
            cols = pl.ds(pl.multiple_of(c * step, step), step)
            block = jnp.concatenate(
                [rows_buf[p, :, :, :, :, cols].reshape(tokens, step) for p in (hw, after)], axis=0
            )
            factor = jnp.concatenate([scaled[hw], scaled[after]], axis=1)
            more = jnp.dot(factor, block, preferred_element_type=F32)
            if last:
                down_buf[:, cols] = (total[:, cols] + more).astype(BF16)
            else:
                total[:, cols] = more

    step4(0)
    far_wait(0)
    far_copy(rows_buf.at[h_first, x_far, y_far, k], 3, h_first, s, ring(h - 1)).start()
    prepare(0)
    z_wait(2)
    step1(2, full)

    @pl.loop(1, SIDE)
    def _(w):
        step3(w)
        step4(w)
        step5(w - 1)

        @pl.when(w < SIDE - 1)
        def _():
            step2(w + 1)

        @pl.when(w == 1)
        def _():
            far_wait(1)
            far_copy(rows_buf.at[source(1), x_far, y_far, k], 2, source(1), s, ring(h + 1)).start()

        @pl.when(w == 2)
        def _():
            drain(meta2.at[0 : SIDE - 1], meta_recv.at[5])

        @pl.when(w > 2)
        def _():
            far_wait(w - 1)

        prepare(w)
        arrived(w - 1)
        scores_of(w - 1, 0)

        @pl.when(w < SIDE - 2)
        def _():
            z_wait(w + 2)
            step1(w + 2, full)

        scores_of(w - 1, 1)
        share(w - 1, 0)
        share(w - 1, 1)

        @pl.when(w < SIDE - 1)
        def _():
            grads_of(w - 1)

        @pl.when(w == 2)
        def _():
            down_of(0, False)

    far_wait(SIDE - 1)
    step5(SIDE - 1)
    arrived(SIDE - 1)
    scores_of(SIDE - 1, 0)
    share(SIDE - 1, 0)
    scores_of(SIDE - 1, 1)
    share(SIDE - 1, 1)
    grads_of(SIDE - 2)
    grads_of(SIDE - 1)
    down_of(SIDE - 2, True)
    slot_out[0] = slot_total[:, 0:128].astype(BF16)
    slot_out[1] = slot_total[:, 128:256].astype(BF16)

    @pl.loop(0, SIDE)
    def _(w):
        sent(w)
        drain(rows_buf.at[0, 0, 0, 0], z_send.at[w])
        drain(rows_buf.at[0, 0, 0, 0], far_send.at[w])

    drain(own_buf, far_sem.at[0])
    drain(meta1.at[0 : 2 * SIDE - 1], meta_send.at[0])
    drain(meta2.at[0 : SIDE * SIDE - 1], meta_send.at[1])

    others = part_recv.at[0 : part_recv.shape[0] - 1]
    drain(others, part_ssem.at[0])
    drain(others, part_rsem.at[0])
    row8 = lax.broadcasted_iota(jnp.int32, (8, 128), 0)
    result = jnp.zeros((8, 128), F32)
    for m in range(2 * SIDE):
        share_sum = part_recv[m * SIDE * SIDE]
        for j in range(1, SIDE * SIDE):
            share_sum = share_sum + part_recv[m * SIDE * SIDE + j]
        for pick in range(picks):
            chosen = jnp.where(own_routes[pick : pick + 1] == m, share_sum, 0.0)
            result = result + jnp.where(row8 == pick, chosen, 0.0)
    prob_out[...] = pltpu.roll(result, lax.rem(128 - base, 128), axis=1)[0:picks, 0:TOK]


def publish(slot_in, down_in, prob_in, gate_out, up_out, down_out, prob_out, sem):
    half = down_in.shape[1]
    hidden = down_in.shape[0] // 2
    moves = [
        pltpu.make_async_copy(down_in.at[0:hidden], down_out.at[:, 0:half], sem.at[0]),
        pltpu.make_async_copy(down_in.at[hidden : 2 * hidden], down_out.at[:, half : 2 * half], sem.at[1]),
        pltpu.make_async_copy(slot_in.at[0], gate_out, sem.at[2]),
        pltpu.make_async_copy(slot_in.at[1], up_out, sem.at[3]),
        pltpu.make_async_copy(prob_in, prob_out, sem.at[4]),
    ]
    for move in moves:
        move.start()
    for move in moves:
        move.wait()


def shards(next_grad, routes, probs, down_weight, gate_pre, up_pre):
    sections = lax.axis_size("pipe")
    grad = next_grad[0]
    weight = down_weight[0, 0]
    gate_rows = gate_pre[0, 0]
    slots, hidden = gate_rows.shape
    width = grad.shape[1]
    picks = routes.shape[2]
    half = width // 2
    tokens = SIDE * 128
    vmem = pl.BlockSpec(memory_space=pltpu.VMEM)
    hbm = pl.BlockSpec(memory_space=pl.ANY)
    dma = pltpu.SemaphoreType.DMA
    slot_grads, down_halves, prob_t = pl.pallas_call(
        functools.partial(kernel, sections),
        out_shape=(
            pltpu.VMEM((2, slots, hidden), BF16),
            pltpu.VMEM((2 * hidden, half), BF16),
            pltpu.VMEM((picks, TOK), F32),
        ),
        in_specs=[vmem, vmem, vmem, hbm, hbm, hbm],
        out_specs=(vmem, vmem, vmem),
        scratch_shapes=[
            pltpu.VMEM((SIDE, SIDE, SIDE, 2, ROWS, half), BF16),
            pltpu.VMEM((ROWS, half), BF16),
            pltpu.VMEM((ROWS, half), BF16),
            pltpu.VMEM((2 * hidden, half), BF16),
            pltpu.VMEM((2, slots, hidden), BF16),
            pltpu.VMEM((2 * hidden, slots), BF16),
            pltpu.VMEM((2 * SIDE, ROWS, 128), BF16),
            pltpu.VMEM((SIDE * SIDE, ROWS, 128), BF16),
            pltpu.VMEM((SIDE, slots, tokens), BF16),
            pltpu.VMEM((SIDE, hidden, tokens), F32),
            pltpu.VMEM((SIDE, hidden, tokens), F32),
            pltpu.VMEM((SIDE, hidden, tokens), F32),
            pltpu.VMEM((SIDE, 2 * hidden, tokens), BF16),
            pltpu.VMEM((2 * hidden, half), F32),
            pltpu.VMEM((slots, 2 * hidden), F32),
            pltpu.VMEM((SIDE, hidden, tokens), F32),
            pltpu.VMEM((SIDE, SIDE, 1, 128), F32),
            pltpu.VMEM((2 * SIDE * SIDE * SIDE, 1, 128), F32),
            dma((SIDE + 1,)),
            dma((SIDE, 4)),
            dma((SIDE, 2)),
            dma((SIDE, 4, 3)),
            dma((SIDE, 2)),
            dma((SIDE,)),
            dma((SIDE,)),
            dma((SIDE,)),
            dma((SIDE,)),
            dma((SIDE,)),
            dma((SIDE,)),
            dma((SIDE,)),
            dma((2,)),
            dma((6,)),
            dma((1,)),
            dma((1,)),
            dma((4,)),
            dma((2,)),
            dma((SIDE,)),
            dma((SIDE,)),
        ],
        compiler_params=pltpu.CompilerParams(
            collective_id=0, has_side_effects=True, vmem_limit_bytes=52 * 1024 * 1024
        ),
        cost_estimate=pl.CostEstimate(
            flops=4 * slots * hidden * width, bytes_accessed=4 * hidden * width, transcendentals=slots * hidden
        ),
    )(grad, routes[0].T, probs[0].T, weight, gate_rows, up_pre[0, 0])
    gate_grad, up_grad, down_grad, prob_grad = pl.pallas_call(
        publish,
        out_shape=(
            jax.ShapeDtypeStruct((slots, hidden), BF16),
            jax.ShapeDtypeStruct((slots, hidden), BF16),
            jax.ShapeDtypeStruct((hidden, width), BF16),
            jax.ShapeDtypeStruct((picks, TOK), F32),
        ),
        in_specs=[vmem, vmem, vmem],
        out_specs=(hbm, hbm, hbm, hbm),
        scratch_shapes=[dma((5,))],
        compiler_params=pltpu.CompilerParams(vmem_limit_bytes=1024 * 1024),
    )(slot_grads, down_halves, prob_t)
    return (gate_grad[None, None], up_grad[None, None], down_grad[None, None], prob_grad.T[None])


def solution(mesh):
    return jax.shard_map(
        shards,
        mesh=mesh,
        in_specs=(
            P("pipe", ("node", "local"), None),
            P("pipe", ("node", "local"), None),
            P("pipe", ("node", "local"), None),
            P("pipe", "node", "local", None),
            P("pipe", "node", None, "local"),
            P("pipe", "node", None, "local"),
        ),
        out_specs=(
            P("pipe", "node", None, "local"),
            P("pipe", "node", None, "local"),
            P("pipe", "node", "local", None),
            P("pipe", ("node", "local"), None),
        ),
        check_vma=False,
    )
```

```python
import functools

import jax
import jax.numpy as jnp
from jax import lax
from jax.experimental import pallas as pl
from jax.experimental.pallas import tpu as pltpu
from jax.sharding import PartitionSpec as P

MESH = pl.DeviceIdType.MESH
F32 = jnp.float32
BF16 = jnp.bfloat16
SIDE = 4
CAP = 5
TOK = 8
ROWS = 16
NT = (((1,), (1,)), ((), ()))


def kernel(
    sections,
    grad_ref,
    routes_ref,
    probs_ref,
    weight_hbm,
    gate_hbm,
    up_hbm,
    slot_out,
    down_buf,
    prob_out,
    rows_buf,
    own_buf,
    far_buf,
    weight_buf,
    pre_buf,
    pre_t,
    meta1,
    meta2,
    select,
    hid,
    gate_f,
    up_f,
    scaled,
    slot_total,
    score_buf,
    part_send,
    part_recv,
    z_recv,
    s1_recv,
    s2_recv,
    s3_recv,
    s4_recv,
    sib_recv,
    z_send,
    s1_send,
    s2_send,
    s3_send,
    s4_send,
    sib_send,
    meta_send,
    meta_recv,
    part_ssem,
    part_rsem,
    load_sem,
    far_sem,
    far_send,
    far_recv,
):
    half = rows_buf.shape[-1]
    mid = half // 2
    quarter = mid // 2
    s = lax.axis_index("pipe")
    node = lax.axis_index("node")
    local = lax.axis_index("local")
    h, k = node // 2, lax.rem(node, 2)
    x, y = local // SIDE, lax.rem(local, SIDE)

    def ring(value):
        return lax.rem(value + 2 * SIDE, SIDE)

    def at(section, plane, core, px, py):
        return {"pipe": section, "node": plane * 2 + core, "local": px * SIDE + py}

    def remote(src, dst, ssem, rsem, device):
        return pltpu.make_async_remote_copy(
            src_ref=src, dst_ref=dst, send_sem=ssem, recv_sem=rsem, device_id=device, device_id_type=MESH
        )

    def send(ref, ssem, rsem, device):
        remote(ref, ref, ssem, rsem, device).start()

    def drain(ref, sem):
        pltpu.make_async_copy(ref, ref, sem).wait()

    s_up = lax.rem(s + 1, sections)
    s_down = lax.rem(s + sections - 1, sections)
    h_first = ring(h + jnp.where(s == sections - 1, 1, 0))
    h_back = ring(h - jnp.where(s == 0, 1, 0))

    line = y * 2 + k
    me = node * SIDE * SIDE + local
    grid = h * SIDE + x

    def line_peer(j):
        other = lax.rem(line + j, 2 * SIDE)
        return at(s, h, lax.rem(other, 2), x, other // 2)

    def plane_peer(j):
        return at(s, h, k, ring(x + j), y)

    planes = (at(s, ring(h + 1), k, x, y), at(s, ring(h - 1), k, x, y))

    barrier = pltpu.get_barrier_semaphore()

    def greet(device):
        pl.semaphore_signal(barrier, inc=1, device_id=device, device_id_type=MESH)

    greet(at(s_up, h_first, k, x, y))
    greet(at(s_up, ring(h_first - 1), k, x, y))

    @pl.loop(1, 2 * SIDE)
    def _(j):
        greet(line_peer(j))

    for j in range(1, SIDE):
        greet(plane_peer(j))
    for device in planes:
        greet(device)
    diagonal = at(s, h, k, ring(x + 2), ring(y + 2))
    greet(diagonal)

    own_buf[0:TOK, :] = grad_ref[:, 0:half]
    own_buf[TOK:ROWS, :] = grad_ref[:, half : 2 * half]

    pl.semaphore_wait(barrier, 2 + (2 * SIDE - 1) + (SIDE - 1) + 2 + 1)

    def z_copy(src, wave, hsrc, section, plane):
        return remote(
            src, rows_buf.at[hsrc, x, y, k], z_send.at[wave], z_recv.at[wave], at(section, plane, k, x, y)
        )

    halves = (pl.ds(0, mid), pl.ds(mid, mid))
    for i in range(2):
        remote(
            own_buf.at[:, halves[i]],
            rows_buf.at[h, x, y, k, :, halves[i]],
            z_send.at[0],
            z_recv.at[SIDE * i],
            at(s_down, h_back, k, x, y),
        ).start()
    z_copy(own_buf, 1, h, s_down, ring(h_back + 1)).start()
    remote(own_buf, far_buf, far_sem.at[0], far_sem.at[1], diagonal).start()

    loads = [
        pltpu.make_async_copy(gate_hbm, pre_buf.at[0], load_sem.at[0]),
        pltpu.make_async_copy(up_hbm, pre_buf.at[1], load_sem.at[1]),
        pltpu.make_async_copy(weight_hbm.at[:, 0:half], weight_buf.at[0:128], load_sem.at[2]),
        pltpu.make_async_copy(weight_hbm.at[:, half : 2 * half], weight_buf.at[128:256], load_sem.at[3]),
    ]
    for load in loads:
        load.start()

    base = y * 32 + k * ROWS
    lane = lax.broadcasted_iota(jnp.int32, (TOK, 128), 1)
    token = lax.broadcasted_iota(jnp.int32, (TOK, 128), 0)
    place_own = jnp.where(lane - base == token, 1.0, 0.0).astype(BF16)
    own_routes = jnp.dot(routes_ref[...].astype(F32).astype(BF16), place_own, preferred_element_type=F32)
    own_probs = jnp.dot(probs_ref[...], place_own, preferred_element_type=F32)
    picks = own_routes.shape[0]
    row16 = lax.broadcasted_iota(jnp.int32, (ROWS, 128), 0).astype(F32)
    tile = jnp.zeros((ROWS, 128), F32)
    for pick in range(picks):
        tile = tile + jnp.where(own_routes[pick : pick + 1] == row16, own_probs[pick : pick + 1], 0.0)
    meta1[line] = tile.astype(BF16)

    @pl.loop(1, 2 * SIDE)
    def _(j):
        send(meta1.at[line], meta_send.at[0], meta_recv.at[0], line_peer(j))

    swap = jnp.where(s == sections - 1, 1, 0)

    def offset(wave):
        return jnp.where(wave == 2, 2 + swap, jnp.where(wave == 3, 3 - swap, wave))

    def source(wave):
        return lax.rem(h_first + SIDE - offset(wave), SIDE)

    def z_wait(wave):
        hw = source(wave)
        drain(rows_buf.at[hw, x, y, k], z_recv.at[offset(wave)])

    left, right = (0, mid), (mid, mid)

    def part(cols, piece):
        return pl.ds(cols[0] + piece * quarter, quarter)

    def blk(hw, px, py, cols):
        return rows_buf.at[hw, px, py, k, :, cols]

    lcols, rcols = halves
    full = pl.ds(0, half)
    x_up, x_down, x_far = ring(x + 1), ring(x - 1), ring(x + 2)
    y_up, y_down, y_far = ring(y + 1), ring(y - 1), ring(y + 2)
    dev_x = (at(s, h, k, x_up, y), at(s, h, k, x_down, y))
    dev_y = (at(s, h, k, x, y_up), at(s, h, k, x, y_down))
    sibling = at(s, h, 1 - k, x, y)
    from_x, from_y = (x_down, x_up, x_far), (y_down, y_up, y_far)

    def hand(ref, w):
        send(ref, sib_send.at[w], sib_recv.at[w], sibling)

    def step1(w, cols):
        mine = blk(source(w), x, y, cols)
        for d in range(2):
            send(mine, s1_send.at[w], s1_recv.at[w, d], dev_x[d])
            send(mine, s1_send.at[w], s1_recv.at[w, 2 + d], dev_y[d])

    def step2(w):
        hw = source(w)
        for d in range(2):
            drain(blk(hw, from_x[d], y, full), s1_recv.at[w, d])
            send(blk(hw, from_x[d], y, halves[d]), s2_send.at[w], s2_recv.at[w, 0], dev_x[d])
            for e in range(2):
                send(blk(hw, from_x[d], y, lcols), s3_send.at[w], s3_recv.at[w, e, d], dev_y[e])
            drain(blk(hw, x, from_y[d], full), s1_recv.at[w, 2 + d])
            send(blk(hw, x, from_y[d], halves[d]), s2_send.at[w], s2_recv.at[w, 1], dev_y[d])
            for e in range(2):
                send(blk(hw, x, from_y[d], rcols), s3_send.at[w], s3_recv.at[w, 2 + e, d], dev_x[e])
        for d in range(2):
            hand(blk(hw, from_x[d], y, full), w)
            hand(blk(hw, x, from_y[d], full), w)

    def step3(w):
        hw = source(w)
        drain(blk(hw, x_far, y, full), s2_recv.at[w, 0])
        for e in range(2):
            send(blk(hw, x_far, y, lcols), s3_send.at[w], s3_recv.at[w, e, 2], dev_y[e])
        drain(blk(hw, x, y_far, full), s2_recv.at[w, 1])
        for e in range(2):
            send(blk(hw, x, y_far, rcols), s3_send.at[w], s3_recv.at[w, 2 + e, 2], dev_x[e])
        hand(blk(hw, x_far, y, full), w)
        hand(blk(hw, x, y_far, full), w)

    def step4(w):
        hw = source(w)
        for j in range(2):
            for e in range(2):
                drain(blk(hw, from_x[j], from_y[e], lcols), s3_recv.at[w, e, j])
                send(blk(hw, from_x[j], from_y[e], part(left, e)), s4_send.at[w], s4_recv.at[w, 0], dev_y[e])
                drain(blk(hw, from_x[e], from_y[j], rcols), s3_recv.at[w, 2 + e, j])
                send(blk(hw, from_x[e], from_y[j], part(right, e)), s4_send.at[w], s4_recv.at[w, 1], dev_x[e])
        hand(blk(hw, x, y, full), w)
        for j in range(2):
            for e in range(2):
                hand(blk(hw, from_x[j], from_y[e], lcols), w)
                hand(blk(hw, from_x[e], from_y[j], rcols), w)

    def step5(w):
        hw = source(w)
        for e in range(2):
            drain(blk(hw, x_far, from_y[e], lcols), s3_recv.at[w, e, 2])
            hand(blk(hw, x_far, from_y[e], lcols), w)
            drain(blk(hw, from_x[e], y_far, rcols), s3_recv.at[w, 2 + e, 2])
            hand(blk(hw, from_x[e], y_far, rcols), w)
        drain(rows_buf.at[hw, 0:2, y_far, k, :, lcols], s4_recv.at[w, 0])
        drain(rows_buf.at[hw, x_far, 0:2, k, :, rcols], s4_recv.at[w, 1])
        for j in range(2):
            hand(blk(hw, from_x[j], y_far, lcols), w)
            hand(blk(hw, x_far, from_y[j], rcols), w)

    def far_copy(src, index, hsrc, section, plane):
        return remote(
            src,
            rows_buf.at[hsrc, x_far, y_far, k],
            far_send.at[index],
            far_recv.at[index],
            at(section, plane, k, x, y),
        )

    def far_wait(w):
        hw = source(w)
        drain(rows_buf.at[hw, x_far, y_far, k], far_recv.at[offset(w)])
        hand(rows_buf.at[hw, x_far, y_far, k], w)

    def arrived(w):
        drain(rows_buf.at[source(w), :, :, 1 - k], sib_recv.at[w])

    def sent(w):
        drain(rows_buf.at[0, 0, :, 0], s1_send.at[w])
        drain(rows_buf.at[0, 0, 0:2, 0], s2_send.at[w])
        drain(rows_buf.at[0, 0:3, 0:2, 0], s3_send.at[w])
        drain(rows_buf.at[0, 0, 0:2, 0], s4_send.at[w])
        drain(rows_buf.at[0, :, :, 0], sib_send.at[w])

    for i in range(2):
        drain(rows_buf.at[h_first, x, y, k, :, halves[i]], z_recv.at[SIDE * i])
        step1(0, halves[i])
    z_copy(rows_buf.at[h_first, x, y, k], 3, h_first, s, ring(h - 1)).start()

    drain(meta1.at[0 : 2 * SIDE - 1], meta_recv.at[0])
    meta2[grid] = jnp.sum(meta1[...].astype(F32), axis=0).astype(BF16)

    def pass_on(tile, kind):
        for j in range(1, SIDE):
            send(meta2.at[tile], meta_send.at[1], meta_recv.at[kind], plane_peer(j))

    above, below, across = ring(h + 1) * SIDE + x, ring(h - 1) * SIDE + x, ring(h + 2) * SIDE + x
    for device in planes:
        send(meta2.at[grid], meta_send.at[1], meta_recv.at[1], device)
    pass_on(grid, 2)
    drain(far_buf, far_sem.at[1])
    far_copy(far_buf, 0, h, s_down, h_back).start()
    far_copy(far_buf, 1, h, s_down, ring(h_back + 1)).start()
    step2(0)
    drain(meta2.at[0:2], meta_recv.at[1])
    send(meta2.at[below], meta_send.at[1], meta_recv.at[3], planes[0])
    pass_on(above, 4)
    pass_on(below, 4)
    z_wait(1)
    z_copy(rows_buf.at[source(1), x, y, k], 2, source(1), s, ring(h + 1)).start()
    step1(1, full)
    for load in loads:
        load.wait()
    pre_t[...] = jnp.concatenate([pre_buf[0], pre_buf[1]], axis=1).astype(F32).T.astype(BF16)

    step3(0)
    step2(1)
    drain(meta2.at[0], meta_recv.at[3])
    pass_on(across, 5)
    drain(meta2.at[0 : SIDE - 1], meta_recv.at[2])
    drain(meta2.at[0 : 2 * SIDE - 2], meta_recv.at[4])
    tokens = SIDE * 128
    slots = slot_total.shape[0]

    def prepare(w):
        hw = source(w)
        tiles = jnp.concatenate([meta2[hw * SIDE + j] for j in range(SIDE)], axis=1).astype(F32)
        rows = lax.broadcasted_iota(jnp.int32, (ROWS, tokens), 0)
        prob = jnp.sum(jnp.where(rows == node, tiles, 0.0), axis=0, keepdims=True)
        prob8 = jnp.broadcast_to(prob, (8, tokens))
        hit = jnp.where(prob8 > 0.0, 1.0, 0.0)
        at_lane = lax.broadcasted_iota(jnp.int32, (8, tokens), 1)
        place = lax.rem(at_lane, ROWS)
        rank = jnp.zeros((8, tokens), F32)
        for back in range(1, TOK):
            rank = rank + jnp.where(place >= back, pltpu.roll(hit, back, axis=1), 0.0)
        group = (at_lane // 32) * (2 * SIDE) + 2 * hw + lax.rem(at_lane // ROWS, 2)
        slot = jnp.where(prob8 > 0.0, group * CAP + rank.astype(jnp.int32), -1)[0:1]
        slot_row = lax.broadcasted_iota(jnp.int32, (slots, tokens), 0)
        select[hw] = jnp.where(slot_row == slot, 1.0, 0.0).astype(BF16)
        moved = jnp.dot(pre_t[...], select[hw], preferred_element_type=F32)
        gate, up = moved[0:128], moved[128:256]
        sig = 1.0 / (1.0 + jnp.exp(-gate))
        act = gate * sig
        hidden = act * up
        hid[hw] = hidden
        gate_f[hw] = prob * (up * sig * (1.0 + gate * (1.0 - sig)))
        up_f[hw] = prob * act
        scaled_hidden = prob * hidden
        scaled[hw, 0:128] = scaled_hidden.astype(BF16)
        scaled[hw, 128:256] = pltpu.roll(scaled_hidden, TOK, axis=1).astype(BF16)

    def scores_of(w, j):
        hw = source(w)
        block = rows_buf[hw, pl.ds(2 * j, 2)].reshape(256, half)
        both = lax.dot_general(weight_buf[...], block, NT, preferred_element_type=F32)
        scores = both[0:128] + pltpu.roll(both[128:256], 256 - TOK, axis=1)
        cols = pl.ds(j * 256, 256)
        shares = jnp.sum(hid[hw, :, cols] * scores, axis=0, keepdims=True)
        part_send[hw, 2 * j] = shares[:, 0:128]
        part_send[hw, 2 * j + 1] = shares[:, 128:256]
        score_buf[hw, :, cols] = scores

    def share(w, j):
        hw = source(w)
        for px in (2 * j, 2 * j + 1):
            for py in range(SIDE):
                for core in range(2):
                    own = (hw == h) & (px == x) & (py == y) & (core == k)

                    @pl.when(own)
                    def _():
                        part_recv[me] = part_send[hw, px]

                    @pl.when(jnp.logical_not(own))
                    def _():
                        remote(
                            part_send.at[hw, px],
                            part_recv.at[me],
                            part_ssem.at[0],
                            part_rsem.at[0],
                            at(s, hw, core, px, py),
                        ).start()

    def grads_of(w):
        hw = source(w)
        d_gate = (gate_f[hw] * score_buf[hw]).astype(BF16)
        d_up = (up_f[hw] * score_buf[hw]).astype(BF16)
        moved = lax.dot_general(
            select[hw], jnp.concatenate([d_gate, d_up], axis=0), NT, preferred_element_type=F32
        )

        @pl.when(w == 0)
        def _():
            slot_total[...] = moved

        @pl.when(w > 0)
        def _():
            slot_total[...] += moved

    def down_all():
        step = half // 4
        factor = jnp.concatenate([scaled[p] for p in range(SIDE)], axis=1)

        @pl.loop(0, half // step)
        def _(c):
            cols = pl.ds(pl.multiple_of(c * step, step), step)
            block = rows_buf[:, :, :, :, :, cols].reshape(SIDE * tokens, step)
            down_buf[:, cols] = jnp.dot(factor, block, preferred_element_type=F32).astype(BF16)

    step4(0)
    far_wait(0)
    far_copy(rows_buf.at[h_first, x_far, y_far, k], 3, h_first, s, ring(h - 1)).start()
    prepare(0)
    z_wait(2)
    step1(2, full)

    @pl.loop(1, SIDE)
    def _(w):
        step3(w)
        step4(w)
        step5(w - 1)

        @pl.when(w < SIDE - 1)
        def _():
            step2(w + 1)

        @pl.when(w == 1)
        def _():
            far_wait(1)
            far_copy(rows_buf.at[source(1), x_far, y_far, k], 2, source(1), s, ring(h + 1)).start()

        @pl.when(w == 2)
        def _():
            drain(meta2.at[0 : SIDE - 1], meta_recv.at[5])

        @pl.when(w > 2)
        def _():
            far_wait(w - 1)

        prepare(w)
        arrived(w - 1)
        scores_of(w - 1, 0)

        @pl.when(w < SIDE - 2)
        def _():
            z_wait(w + 2)
            step1(w + 2, full)

        scores_of(w - 1, 1)
        share(w - 1, 0)
        share(w - 1, 1)

        @pl.when(w < SIDE - 1)
        def _():
            grads_of(w - 1)

    far_wait(SIDE - 1)
    step5(SIDE - 1)
    arrived(SIDE - 1)
    scores_of(SIDE - 1, 0)
    share(SIDE - 1, 0)
    scores_of(SIDE - 1, 1)
    share(SIDE - 1, 1)
    grads_of(SIDE - 2)
    grads_of(SIDE - 1)
    down_all()
    slot_out[0] = slot_total[:, 0:128].astype(BF16)
    slot_out[1] = slot_total[:, 128:256].astype(BF16)

    @pl.loop(0, SIDE)
    def _(w):
        sent(w)
        drain(rows_buf.at[0, 0, 0, 0], z_send.at[w])
        drain(rows_buf.at[0, 0, 0, 0], far_send.at[w])

    drain(own_buf, far_sem.at[0])
    drain(meta1.at[0 : 2 * SIDE - 1], meta_send.at[0])
    drain(meta2.at[0 : SIDE * SIDE - 1], meta_send.at[1])

    others = part_recv.at[0 : part_recv.shape[0] - 1]
    drain(others, part_ssem.at[0])
    drain(others, part_rsem.at[0])
    row8 = lax.broadcasted_iota(jnp.int32, (8, 128), 0)
    result = jnp.zeros((8, 128), F32)
    for m in range(2 * SIDE):
        share_sum = part_recv[m * SIDE * SIDE]
        for j in range(1, SIDE * SIDE):
            share_sum = share_sum + part_recv[m * SIDE * SIDE + j]
        for pick in range(picks):
            chosen = jnp.where(own_routes[pick : pick + 1] == m, share_sum, 0.0)
            result = result + jnp.where(row8 == pick, chosen, 0.0)
    prob_out[...] = pltpu.roll(result, lax.rem(128 - base, 128), axis=1)[0:picks, 0:TOK]


def publish(slot_in, down_in, prob_in, gate_out, up_out, down_out, prob_out, sem):
    half = down_in.shape[1]
    hidden = down_in.shape[0] // 2
    moves = [
        pltpu.make_async_copy(down_in.at[0:hidden], down_out.at[:, 0:half], sem.at[0]),
        pltpu.make_async_copy(down_in.at[hidden : 2 * hidden], down_out.at[:, half : 2 * half], sem.at[1]),
        pltpu.make_async_copy(slot_in.at[0], gate_out, sem.at[2]),
        pltpu.make_async_copy(slot_in.at[1], up_out, sem.at[3]),
        pltpu.make_async_copy(prob_in, prob_out, sem.at[4]),
    ]
    for move in moves:
        move.start()
    for move in moves:
        move.wait()


def shards(next_grad, routes, probs, down_weight, gate_pre, up_pre):
    sections = lax.axis_size("pipe")
    grad = next_grad[0]
    weight = down_weight[0, 0]
    gate_rows = gate_pre[0, 0]
    slots, hidden = gate_rows.shape
    width = grad.shape[1]
    picks = routes.shape[2]
    half = width // 2
    tokens = SIDE * 128
    vmem = pl.BlockSpec(memory_space=pltpu.VMEM)
    hbm = pl.BlockSpec(memory_space=pl.ANY)
    dma = pltpu.SemaphoreType.DMA
    slot_grads, down_halves, prob_t = pl.pallas_call(
        functools.partial(kernel, sections),
        out_shape=(
            pltpu.VMEM((2, slots, hidden), BF16),
            pltpu.VMEM((2 * hidden, half), BF16),
            pltpu.VMEM((picks, TOK), F32),
        ),
        in_specs=[vmem, vmem, vmem, hbm, hbm, hbm],
        out_specs=(vmem, vmem, vmem),
        scratch_shapes=[
            pltpu.VMEM((SIDE, SIDE, SIDE, 2, ROWS, half), BF16),
            pltpu.VMEM((ROWS, half), BF16),
            pltpu.VMEM((ROWS, half), BF16),
            pltpu.VMEM((2 * hidden, half), BF16),
            pltpu.VMEM((2, slots, hidden), BF16),
            pltpu.VMEM((2 * hidden, slots), BF16),
            pltpu.VMEM((2 * SIDE, ROWS, 128), BF16),
            pltpu.VMEM((SIDE * SIDE, ROWS, 128), BF16),
            pltpu.VMEM((SIDE, slots, tokens), BF16),
            pltpu.VMEM((SIDE, hidden, tokens), F32),
            pltpu.VMEM((SIDE, hidden, tokens), F32),
            pltpu.VMEM((SIDE, hidden, tokens), F32),
            pltpu.VMEM((SIDE, 2 * hidden, tokens), BF16),
            pltpu.VMEM((slots, 2 * hidden), F32),
            pltpu.VMEM((SIDE, hidden, tokens), F32),
            pltpu.VMEM((SIDE, SIDE, 1, 128), F32),
            pltpu.VMEM((2 * SIDE * SIDE * SIDE, 1, 128), F32),
            dma((SIDE + 1,)),
            dma((SIDE, 4)),
            dma((SIDE, 2)),
            dma((SIDE, 4, 3)),
            dma((SIDE, 2)),
            dma((SIDE,)),
            dma((SIDE,)),
            dma((SIDE,)),
            dma((SIDE,)),
            dma((SIDE,)),
            dma((SIDE,)),
            dma((SIDE,)),
            dma((2,)),
            dma((6,)),
            dma((1,)),
            dma((1,)),
            dma((4,)),
            dma((2,)),
            dma((SIDE,)),
            dma((SIDE,)),
        ],
        compiler_params=pltpu.CompilerParams(
            collective_id=0, has_side_effects=True, vmem_limit_bytes=52 * 1024 * 1024
        ),
        cost_estimate=pl.CostEstimate(
            flops=4 * slots * hidden * width, bytes_accessed=4 * hidden * width, transcendentals=slots * hidden
        ),
    )(grad, routes[0].T, probs[0].T, weight, gate_rows, up_pre[0, 0])
    gate_grad, up_grad, down_grad, prob_grad = pl.pallas_call(
        publish,
        out_shape=(
            jax.ShapeDtypeStruct((slots, hidden), BF16),
            jax.ShapeDtypeStruct((slots, hidden), BF16),
            jax.ShapeDtypeStruct((hidden, width), BF16),
            jax.ShapeDtypeStruct((picks, TOK), F32),
        ),
        in_specs=[vmem, vmem, vmem],
        out_specs=(hbm, hbm, hbm, hbm),
        scratch_shapes=[dma((5,))],
        compiler_params=pltpu.CompilerParams(vmem_limit_bytes=1024 * 1024),
    )(slot_grads, down_halves, prob_t)
    return (gate_grad[None, None], up_grad[None, None], down_grad[None, None], prob_grad.T[None])


def solution(mesh):
    return jax.shard_map(
        shards,
        mesh=mesh,
        in_specs=(
            P("pipe", ("node", "local"), None),
            P("pipe", ("node", "local"), None),
            P("pipe", ("node", "local"), None),
            P("pipe", "node", "local", None),
            P("pipe", "node", None, "local"),
            P("pipe", "node", None, "local"),
        ),
        out_specs=(
            P("pipe", "node", None, "local"),
            P("pipe", "node", None, "local"),
            P("pipe", "node", "local", None),
            P("pipe", ("node", "local"), None),
        ),
        check_vma=False,
    )
```

```python
import functools

import jax
import jax.numpy as jnp
from jax import lax
from jax.experimental import pallas as pl
from jax.experimental.pallas import tpu as pltpu
from jax.sharding import PartitionSpec as P

MESH = pl.DeviceIdType.MESH
F32 = jnp.float32
BF16 = jnp.bfloat16
SIDE = 4
CAP = 5
TOK = 8
ROWS = 16
NT = (((1,), (1,)), ((), ()))


def kernel(
    sections,
    grad_ref,
    routes_ref,
    probs_ref,
    weight_hbm,
    gate_hbm,
    up_hbm,
    slot_out,
    down_buf,
    prob_out,
    rows_buf,
    own_buf,
    far_buf,
    weight_buf,
    pre_buf,
    pre_t,
    meta1,
    meta2,
    select,
    hid,
    gate_f,
    up_f,
    scaled,
    slot_total,
    score_buf,
    part_send,
    part_recv,
    z_recv,
    s1_recv,
    s2_recv,
    s3_recv,
    s4_recv,
    sib_recv,
    z_send,
    s1_send,
    s2_send,
    s3_send,
    s4_send,
    sib_send,
    meta_send,
    meta_recv,
    part_ssem,
    part_rsem,
    load_sem,
    far_sem,
    far_send,
    far_recv,
):
    half = rows_buf.shape[-1]
    mid = half // 2
    quarter = mid // 2
    s = lax.axis_index("pipe")
    node = lax.axis_index("node")
    local = lax.axis_index("local")
    h, k = node // 2, lax.rem(node, 2)
    x, y = local // SIDE, lax.rem(local, SIDE)

    def ring(value):
        return lax.rem(value + 2 * SIDE, SIDE)

    def at(section, plane, core, px, py):
        return {"pipe": section, "node": plane * 2 + core, "local": px * SIDE + py}

    def remote(src, dst, ssem, rsem, device):
        return pltpu.make_async_remote_copy(
            src_ref=src, dst_ref=dst, send_sem=ssem, recv_sem=rsem, device_id=device, device_id_type=MESH
        )

    def send(ref, ssem, rsem, device):
        remote(ref, ref, ssem, rsem, device).start()

    def drain(ref, sem):
        pltpu.make_async_copy(ref, ref, sem).wait()

    s_up = lax.rem(s + 1, sections)
    s_down = lax.rem(s + sections - 1, sections)
    h_first = ring(h + jnp.where(s == sections - 1, 1, 0))
    h_back = ring(h - jnp.where(s == 0, 1, 0))

    line = y * 2 + k
    me = node * SIDE * SIDE + local
    grid = h * SIDE + x

    def line_peer(j):
        other = lax.rem(line + j, 2 * SIDE)
        return at(s, h, lax.rem(other, 2), x, other // 2)

    def plane_peer(j):
        return at(s, h, k, ring(x + j), y)

    planes = (at(s, ring(h + 1), k, x, y), at(s, ring(h - 1), k, x, y))

    barrier = pltpu.get_barrier_semaphore()

    def greet(device):
        pl.semaphore_signal(barrier, inc=1, device_id=device, device_id_type=MESH)

    greet(at(s_up, h_first, k, x, y))
    greet(at(s_up, ring(h_first - 1), k, x, y))

    @pl.loop(1, 2 * SIDE)
    def _(j):
        greet(line_peer(j))

    for j in range(1, SIDE):
        greet(plane_peer(j))
    for device in planes:
        greet(device)
    diagonal = at(s, h, k, ring(x + 2), ring(y + 2))
    greet(diagonal)

    own_buf[0:TOK, :] = grad_ref[:, 0:half]
    own_buf[TOK:ROWS, :] = grad_ref[:, half : 2 * half]

    pl.semaphore_wait(barrier, 2 + (2 * SIDE - 1) + (SIDE - 1) + 2 + 1)

    def z_copy(src, wave, hsrc, section, plane):
        return remote(
            src, rows_buf.at[hsrc, x, y, k], z_send.at[wave], z_recv.at[wave], at(section, plane, k, x, y)
        )

    halves = (pl.ds(0, mid), pl.ds(mid, mid))
    for i in range(2):
        remote(
            own_buf.at[:, halves[i]],
            rows_buf.at[h, x, y, k, :, halves[i]],
            z_send.at[0],
            z_recv.at[SIDE * i],
            at(s_down, h_back, k, x, y),
        ).start()
    z_copy(own_buf, 1, h, s_down, ring(h_back + 1)).start()
    remote(own_buf, far_buf, far_sem.at[0], far_sem.at[1], diagonal).start()

    loads = [
        pltpu.make_async_copy(gate_hbm, pre_buf.at[0], load_sem.at[0]),
        pltpu.make_async_copy(up_hbm, pre_buf.at[1], load_sem.at[1]),
        pltpu.make_async_copy(weight_hbm.at[:, 0:half], weight_buf.at[0:128], load_sem.at[2]),
        pltpu.make_async_copy(weight_hbm.at[:, half : 2 * half], weight_buf.at[128:256], load_sem.at[3]),
    ]
    for load in loads:
        load.start()

    base = y * 32 + k * ROWS
    lane = lax.broadcasted_iota(jnp.int32, (TOK, 128), 1)
    token = lax.broadcasted_iota(jnp.int32, (TOK, 128), 0)
    place_own = jnp.where(lane - base == token, 1.0, 0.0).astype(BF16)
    own_routes = jnp.dot(routes_ref[...].astype(F32).astype(BF16), place_own, preferred_element_type=F32)
    own_probs = jnp.dot(probs_ref[...], place_own, preferred_element_type=F32)
    picks = own_routes.shape[0]
    row16 = lax.broadcasted_iota(jnp.int32, (ROWS, 128), 0).astype(F32)
    tile = jnp.zeros((ROWS, 128), F32)
    for pick in range(picks):
        tile = tile + jnp.where(own_routes[pick : pick + 1] == row16, own_probs[pick : pick + 1], 0.0)
    meta1[line] = tile.astype(BF16)

    @pl.loop(1, 2 * SIDE)
    def _(j):
        send(meta1.at[line], meta_send.at[0], meta_recv.at[0], line_peer(j))

    swap = jnp.where(s == sections - 1, 1, 0)

    def offset(wave):
        return jnp.where(wave == 2, 2 + swap, jnp.where(wave == 3, 3 - swap, wave))

    def source(wave):
        return lax.rem(h_first + SIDE - offset(wave), SIDE)

    def z_wait(wave):
        hw = source(wave)
        drain(rows_buf.at[hw, x, y, k], z_recv.at[offset(wave)])

    left, right = (0, mid), (mid, mid)

    def part(cols, piece):
        return pl.ds(cols[0] + piece * quarter, quarter)

    def blk(hw, px, py, cols):
        return rows_buf.at[hw, px, py, k, :, cols]

    lcols, rcols = halves
    full = pl.ds(0, half)
    x_up, x_down, x_far = ring(x + 1), ring(x - 1), ring(x + 2)
    y_up, y_down, y_far = ring(y + 1), ring(y - 1), ring(y + 2)
    dev_x = (at(s, h, k, x_up, y), at(s, h, k, x_down, y))
    dev_y = (at(s, h, k, x, y_up), at(s, h, k, x, y_down))
    sibling = at(s, h, 1 - k, x, y)
    from_x, from_y = (x_down, x_up, x_far), (y_down, y_up, y_far)

    def hand(ref, w):
        send(ref, sib_send.at[w], sib_recv.at[w], sibling)

    def step1(w, cols):
        mine = blk(source(w), x, y, cols)
        for d in range(2):
            send(mine, s1_send.at[w], s1_recv.at[w, d], dev_x[d])
            send(mine, s1_send.at[w], s1_recv.at[w, 2 + d], dev_y[d])

    def step2(w):
        hw = source(w)
        for d in range(2):
            drain(blk(hw, from_x[d], y, full), s1_recv.at[w, d])
            send(blk(hw, from_x[d], y, halves[d]), s2_send.at[w], s2_recv.at[w, 0], dev_x[d])
            for e in range(2):
                send(blk(hw, from_x[d], y, lcols), s3_send.at[w], s3_recv.at[w, e, d], dev_y[e])
            drain(blk(hw, x, from_y[d], full), s1_recv.at[w, 2 + d])
            send(blk(hw, x, from_y[d], halves[d]), s2_send.at[w], s2_recv.at[w, 1], dev_y[d])
            for e in range(2):
                send(blk(hw, x, from_y[d], rcols), s3_send.at[w], s3_recv.at[w, 2 + e, d], dev_x[e])
        for d in range(2):
            hand(blk(hw, from_x[d], y, full), w)
            hand(blk(hw, x, from_y[d], full), w)

    def step3(w):
        hw = source(w)
        drain(blk(hw, x_far, y, full), s2_recv.at[w, 0])
        for e in range(2):
            send(blk(hw, x_far, y, lcols), s3_send.at[w], s3_recv.at[w, e, 2], dev_y[e])
        drain(blk(hw, x, y_far, full), s2_recv.at[w, 1])
        for e in range(2):
            send(blk(hw, x, y_far, rcols), s3_send.at[w], s3_recv.at[w, 2 + e, 2], dev_x[e])
        hand(blk(hw, x_far, y, full), w)
        hand(blk(hw, x, y_far, full), w)

    def step4(w):
        hw = source(w)
        for j in range(2):
            for e in range(2):
                drain(blk(hw, from_x[j], from_y[e], lcols), s3_recv.at[w, e, j])
                send(blk(hw, from_x[j], from_y[e], part(left, e)), s4_send.at[w], s4_recv.at[w, 0], dev_y[e])
                drain(blk(hw, from_x[e], from_y[j], rcols), s3_recv.at[w, 2 + e, j])
                send(blk(hw, from_x[e], from_y[j], part(right, e)), s4_send.at[w], s4_recv.at[w, 1], dev_x[e])
        hand(blk(hw, x, y, full), w)
        for j in range(2):
            for e in range(2):
                hand(blk(hw, from_x[j], from_y[e], lcols), w)
                hand(blk(hw, from_x[e], from_y[j], rcols), w)

    def step5(w):
        hw = source(w)
        for e in range(2):
            drain(blk(hw, x_far, from_y[e], lcols), s3_recv.at[w, e, 2])
            hand(blk(hw, x_far, from_y[e], lcols), w)
            drain(blk(hw, from_x[e], y_far, rcols), s3_recv.at[w, 2 + e, 2])
            hand(blk(hw, from_x[e], y_far, rcols), w)
        drain(rows_buf.at[hw, 0:2, y_far, k, :, lcols], s4_recv.at[w, 0])
        drain(rows_buf.at[hw, x_far, 0:2, k, :, rcols], s4_recv.at[w, 1])
        for j in range(2):
            hand(blk(hw, from_x[j], y_far, lcols), w)
            hand(blk(hw, x_far, from_y[j], rcols), w)

    def far_copy(src, index, hsrc, section, plane):
        return remote(
            src,
            rows_buf.at[hsrc, x_far, y_far, k],
            far_send.at[index],
            far_recv.at[index],
            at(section, plane, k, x, y),
        )

    def far_wait(w):
        hw = source(w)
        drain(rows_buf.at[hw, x_far, y_far, k], far_recv.at[offset(w)])
        hand(rows_buf.at[hw, x_far, y_far, k], w)

    def arrived(w):
        drain(rows_buf.at[source(w), :, :, 1 - k], sib_recv.at[w])

    def sent(w):
        drain(rows_buf.at[0, 0, :, 0], s1_send.at[w])
        drain(rows_buf.at[0, 0, 0:2, 0], s2_send.at[w])
        drain(rows_buf.at[0, 0:3, 0:2, 0], s3_send.at[w])
        drain(rows_buf.at[0, 0, 0:2, 0], s4_send.at[w])
        drain(rows_buf.at[0, :, :, 0], sib_send.at[w])

    for i in range(2):
        drain(rows_buf.at[h_first, x, y, k, :, halves[i]], z_recv.at[SIDE * i])
        step1(0, halves[i])
    z_copy(rows_buf.at[h_first, x, y, k], 3, h_first, s, ring(h - 1)).start()

    drain(meta1.at[0 : 2 * SIDE - 1], meta_recv.at[0])
    meta2[grid] = jnp.sum(meta1[...].astype(F32), axis=0).astype(BF16)

    def pass_on(tile, kind):
        for j in range(1, SIDE):
            send(meta2.at[tile], meta_send.at[1], meta_recv.at[kind], plane_peer(j))

    above, below, across = ring(h + 1) * SIDE + x, ring(h - 1) * SIDE + x, ring(h + 2) * SIDE + x
    for device in planes:
        send(meta2.at[grid], meta_send.at[1], meta_recv.at[1], device)
    pass_on(grid, 2)
    drain(far_buf, far_sem.at[1])
    far_copy(far_buf, 0, h, s_down, h_back).start()
    far_copy(far_buf, 1, h, s_down, ring(h_back + 1)).start()
    step2(0)
    drain(meta2.at[0:2], meta_recv.at[1])
    send(meta2.at[below], meta_send.at[1], meta_recv.at[3], planes[0])
    pass_on(above, 4)
    pass_on(below, 4)
    z_wait(1)
    z_copy(rows_buf.at[source(1), x, y, k], 2, source(1), s, ring(h + 1)).start()
    step1(1, full)
    for load in loads:
        load.wait()
    pre_t[...] = jnp.concatenate([pre_buf[0], pre_buf[1]], axis=1).astype(F32).T.astype(BF16)

    step3(0)
    step2(1)
    drain(meta2.at[0], meta_recv.at[3])
    pass_on(across, 5)
    drain(meta2.at[0 : SIDE - 1], meta_recv.at[2])
    drain(meta2.at[0 : 2 * SIDE - 2], meta_recv.at[4])
    tokens = SIDE * 128
    slots = slot_total.shape[0]

    def prepare(w):
        hw = source(w)
        tiles = jnp.concatenate([meta2[hw * SIDE + j] for j in range(SIDE)], axis=1).astype(F32)
        rows = lax.broadcasted_iota(jnp.int32, (ROWS, tokens), 0)
        prob = jnp.sum(jnp.where(rows == node, tiles, 0.0), axis=0, keepdims=True)
        prob8 = jnp.broadcast_to(prob, (8, tokens))
        hit = jnp.where(prob8 > 0.0, 1.0, 0.0)
        at_lane = lax.broadcasted_iota(jnp.int32, (8, tokens), 1)
        place = lax.rem(at_lane, ROWS)
        rank = jnp.zeros((8, tokens), F32)
        for back in range(1, TOK):
            rank = rank + jnp.where(place >= back, pltpu.roll(hit, back, axis=1), 0.0)
        group = (at_lane // 32) * (2 * SIDE) + 2 * hw + lax.rem(at_lane // ROWS, 2)
        slot = jnp.where(prob8 > 0.0, group * CAP + rank.astype(jnp.int32), -1)[0:1]
        slot_row = lax.broadcasted_iota(jnp.int32, (slots, tokens), 0)
        select[hw] = jnp.where(slot_row == slot, 1.0, 0.0).astype(BF16)
        moved = jnp.dot(pre_t[...], select[hw], preferred_element_type=F32)
        gate, up = moved[0:128], moved[128:256]
        sig = 1.0 / (1.0 + jnp.exp(-gate))
        act = gate * sig
        hidden = act * up
        hid[hw] = hidden
        gate_f[hw] = prob * (up * sig * (1.0 + gate * (1.0 - sig)))
        up_f[hw] = prob * act
        scaled_hidden = prob * hidden
        scaled[hw, 0:128] = scaled_hidden.astype(BF16)
        scaled[hw, 128:256] = pltpu.roll(scaled_hidden, TOK, axis=1).astype(BF16)

    def scores_of(w, j):
        hw = source(w)
        block = rows_buf[hw, pl.ds(2 * j, 2)].reshape(256, half)
        both = lax.dot_general(weight_buf[...], block, NT, preferred_element_type=F32)
        scores = both[0:128] + pltpu.roll(both[128:256], 256 - TOK, axis=1)
        cols = pl.ds(j * 256, 256)
        shares = jnp.sum(hid[hw, :, cols] * scores, axis=0, keepdims=True)
        part_send[hw, 2 * j] = shares[:, 0:128]
        part_send[hw, 2 * j + 1] = shares[:, 128:256]
        score_buf[hw, :, cols] = scores

    def share(w, j):
        hw = source(w)
        for px in (2 * j, 2 * j + 1):
            for py in range(SIDE):
                for core in range(2):
                    own = (hw == h) & (px == x) & (py == y) & (core == k)

                    @pl.when(own)
                    def _():
                        part_recv[me] = part_send[hw, px]

                    @pl.when(jnp.logical_not(own))
                    def _():
                        remote(
                            part_send.at[hw, px],
                            part_recv.at[me],
                            part_ssem.at[0],
                            part_rsem.at[0],
                            at(s, hw, core, px, py),
                        ).start()

    def grads_of(w):
        hw = source(w)
        d_gate = (gate_f[hw] * score_buf[hw]).astype(BF16)
        d_up = (up_f[hw] * score_buf[hw]).astype(BF16)
        moved = lax.dot_general(
            select[hw], jnp.concatenate([d_gate, d_up], axis=0), NT, preferred_element_type=F32
        )

        @pl.when(w == 0)
        def _():
            slot_total[...] = moved

        @pl.when(w > 0)
        def _():
            slot_total[...] += moved

    def down_all():
        step = half // 4
        factor = jnp.concatenate([scaled[p] for p in range(SIDE)], axis=1)

        @pl.loop(0, half // step)
        def _(c):
            cols = pl.ds(pl.multiple_of(c * step, step), step)
            block = rows_buf[:, :, :, :, :, cols].reshape(SIDE * tokens, step)
            down_buf[:, cols] = jnp.dot(factor, block, preferred_element_type=F32).astype(BF16)

    step4(0)
    far_wait(0)
    far_copy(rows_buf.at[h_first, x_far, y_far, k], 3, h_first, s, ring(h - 1)).start()
    prepare(0)
    z_wait(2)
    step1(2, full)

    @pl.loop(1, SIDE)
    def _(w):
        step3(w)
        step4(w)
        step5(w - 1)

        @pl.when(w < SIDE - 1)
        def _():
            step2(w + 1)

        @pl.when(w == 1)
        def _():
            far_wait(1)
            far_copy(rows_buf.at[source(1), x_far, y_far, k], 2, source(1), s, ring(h + 1)).start()

        @pl.when(w == 2)
        def _():
            drain(meta2.at[0 : SIDE - 1], meta_recv.at[5])

        @pl.when(w > 2)
        def _():
            far_wait(w - 1)

        prepare(w)
        arrived(w - 1)
        scores_of(w - 1, 0)

        @pl.when(w < SIDE - 2)
        def _():
            z_wait(w + 2)
            step1(w + 2, full)

        scores_of(w - 1, 1)
        share(w - 1, 0)
        share(w - 1, 1)

    far_wait(SIDE - 1)
    step5(SIDE - 1)
    arrived(SIDE - 1)
    scores_of(SIDE - 1, 0)
    share(SIDE - 1, 0)
    scores_of(SIDE - 1, 1)
    share(SIDE - 1, 1)

    @pl.loop(0, SIDE)
    def _(w):
        grads_of(w)

    down_all()
    slot_out[0] = slot_total[:, 0:128].astype(BF16)
    slot_out[1] = slot_total[:, 128:256].astype(BF16)

    @pl.loop(0, SIDE)
    def _(w):
        sent(w)
        drain(rows_buf.at[0, 0, 0, 0], z_send.at[w])
        drain(rows_buf.at[0, 0, 0, 0], far_send.at[w])

    drain(own_buf, far_sem.at[0])
    drain(meta1.at[0 : 2 * SIDE - 1], meta_send.at[0])
    drain(meta2.at[0 : SIDE * SIDE - 1], meta_send.at[1])

    others = part_recv.at[0 : part_recv.shape[0] - 1]
    drain(others, part_ssem.at[0])
    drain(others, part_rsem.at[0])
    row8 = lax.broadcasted_iota(jnp.int32, (8, 128), 0)
    result = jnp.zeros((8, 128), F32)
    for m in range(2 * SIDE):
        share_sum = part_recv[m * SIDE * SIDE]
        for j in range(1, SIDE * SIDE):
            share_sum = share_sum + part_recv[m * SIDE * SIDE + j]
        for pick in range(picks):
            chosen = jnp.where(own_routes[pick : pick + 1] == m, share_sum, 0.0)
            result = result + jnp.where(row8 == pick, chosen, 0.0)
    prob_out[...] = pltpu.roll(result, lax.rem(128 - base, 128), axis=1)[0:picks, 0:TOK]


def publish(slot_in, down_in, prob_in, gate_out, up_out, down_out, prob_out, sem):
    half = down_in.shape[1]
    hidden = down_in.shape[0] // 2
    moves = [
        pltpu.make_async_copy(down_in.at[0:hidden], down_out.at[:, 0:half], sem.at[0]),
        pltpu.make_async_copy(down_in.at[hidden : 2 * hidden], down_out.at[:, half : 2 * half], sem.at[1]),
        pltpu.make_async_copy(slot_in.at[0], gate_out, sem.at[2]),
        pltpu.make_async_copy(slot_in.at[1], up_out, sem.at[3]),
        pltpu.make_async_copy(prob_in, prob_out, sem.at[4]),
    ]
    for move in moves:
        move.start()
    for move in moves:
        move.wait()


def shards(next_grad, routes, probs, down_weight, gate_pre, up_pre):
    sections = lax.axis_size("pipe")
    grad = next_grad[0]
    weight = down_weight[0, 0]
    gate_rows = gate_pre[0, 0]
    slots, hidden = gate_rows.shape
    width = grad.shape[1]
    picks = routes.shape[2]
    half = width // 2
    tokens = SIDE * 128
    vmem = pl.BlockSpec(memory_space=pltpu.VMEM)
    hbm = pl.BlockSpec(memory_space=pl.ANY)
    dma = pltpu.SemaphoreType.DMA
    slot_grads, down_halves, prob_t = pl.pallas_call(
        functools.partial(kernel, sections),
        out_shape=(
            pltpu.VMEM((2, slots, hidden), BF16),
            pltpu.VMEM((2 * hidden, half), BF16),
            pltpu.VMEM((picks, TOK), F32),
        ),
        in_specs=[vmem, vmem, vmem, hbm, hbm, hbm],
        out_specs=(vmem, vmem, vmem),
        scratch_shapes=[
            pltpu.VMEM((SIDE, SIDE, SIDE, 2, ROWS, half), BF16),
            pltpu.VMEM((ROWS, half), BF16),
            pltpu.VMEM((ROWS, half), BF16),
            pltpu.VMEM((2 * hidden, half), BF16),
            pltpu.VMEM((2, slots, hidden), BF16),
            pltpu.VMEM((2 * hidden, slots), BF16),
            pltpu.VMEM((2 * SIDE, ROWS, 128), BF16),
            pltpu.VMEM((SIDE * SIDE, ROWS, 128), BF16),
            pltpu.VMEM((SIDE, slots, tokens), BF16),
            pltpu.VMEM((SIDE, hidden, tokens), F32),
            pltpu.VMEM((SIDE, hidden, tokens), F32),
            pltpu.VMEM((SIDE, hidden, tokens), F32),
            pltpu.VMEM((SIDE, 2 * hidden, tokens), BF16),
            pltpu.VMEM((slots, 2 * hidden), F32),
            pltpu.VMEM((SIDE, hidden, tokens), F32),
            pltpu.VMEM((SIDE, SIDE, 1, 128), F32),
            pltpu.VMEM((2 * SIDE * SIDE * SIDE, 1, 128), F32),
            dma((SIDE + 1,)),
            dma((SIDE, 4)),
            dma((SIDE, 2)),
            dma((SIDE, 4, 3)),
            dma((SIDE, 2)),
            dma((SIDE,)),
            dma((SIDE,)),
            dma((SIDE,)),
            dma((SIDE,)),
            dma((SIDE,)),
            dma((SIDE,)),
            dma((SIDE,)),
            dma((2,)),
            dma((6,)),
            dma((1,)),
            dma((1,)),
            dma((4,)),
            dma((2,)),
            dma((SIDE,)),
            dma((SIDE,)),
        ],
        compiler_params=pltpu.CompilerParams(
            collective_id=0, has_side_effects=True, vmem_limit_bytes=52 * 1024 * 1024
        ),
        cost_estimate=pl.CostEstimate(
            flops=4 * slots * hidden * width, bytes_accessed=4 * hidden * width, transcendentals=slots * hidden
        ),
    )(grad, routes[0].T, probs[0].T, weight, gate_rows, up_pre[0, 0])
    gate_grad, up_grad, down_grad, prob_grad = pl.pallas_call(
        publish,
        out_shape=(
            jax.ShapeDtypeStruct((slots, hidden), BF16),
            jax.ShapeDtypeStruct((slots, hidden), BF16),
            jax.ShapeDtypeStruct((hidden, width), BF16),
            jax.ShapeDtypeStruct((picks, TOK), F32),
        ),
        in_specs=[vmem, vmem, vmem],
        out_specs=(hbm, hbm, hbm, hbm),
        scratch_shapes=[dma((5,))],
        compiler_params=pltpu.CompilerParams(vmem_limit_bytes=1024 * 1024),
    )(slot_grads, down_halves, prob_t)
    return (gate_grad[None, None], up_grad[None, None], down_grad[None, None], prob_grad.T[None])


def solution(mesh):
    return jax.shard_map(
        shards,
        mesh=mesh,
        in_specs=(
            P("pipe", ("node", "local"), None),
            P("pipe", ("node", "local"), None),
            P("pipe", ("node", "local"), None),
            P("pipe", "node", "local", None),
            P("pipe", "node", None, "local"),
            P("pipe", "node", None, "local"),
        ),
        out_specs=(
            P("pipe", "node", None, "local"),
            P("pipe", "node", None, "local"),
            P("pipe", "node", "local", None),
            P("pipe", ("node", "local"), None),
        ),
        check_vma=False,
    )
```
